32 devices in a mesh: group: 2 (over x), replica: 16 (over z, y, core).
Axes of the slice: x: 2, y: 2, z: 4, core: 2. Of those that a mesh axis runs over, the one named last changes fastest.
Arguments:
- hidden_in: bfloat16 [10240, 3072], P(('group', 'replica')), may hold values from -8 to 8
- w_query: bfloat16 [3072, 1536], replicated, may hold values from -0.109375 to 0.109375
- query_gain: float32 [128], replicated, may hold values from 0.5 to 2
- down_projection_matrix: bfloat16 [3072, 64], replicated, may hold values from -0.23925781 to 0.23925781
- up_projection_matrix: bfloat16 [64, 1536], replicated, may hold values from -0.59765625 to 0.59765625
- query_cotangent: bfloat16 [10240, 1536], P(('group', 'replica')), may hold values from -8 to 8
- first_moment: float32 [4608, 64], P(('group', 'replica')), may hold values from -3 to 3
- second_moment: float32 [4608, 64], P(('group', 'replica')), may hold values from 0.001 to 0.1
Outputs:
- new_down: bfloat16 [3072, 64], replicated
- new_up: bfloat16 [64, 1536], replicated
- first_next: float32 [4608, 64], P(('group', 'replica'))
- second_next: float32 [4608, 64], P(('group', 'replica'))
The draws below stay inside these ranges and needn't reach their ends.
All inputs are finite; a program needn't handle non-finite values.
Results may differ from the reference program's by a relative error of at most 0.0019.
Values may be sent and summed in bfloat16 or wider, within the bound.
No kernel may reach another device: no remote copies, remote signals or barrier semaphores. Data moves between devices by JAX's collectives and lax.ppermute only.
A program may use at most 64 MiB of HBM per device.

```python
import math
import jax
import jax.numpy as jnp
from jax import lax

D = 3072
HD = 128
QW = 1536
R = 64
TOK_DEV = 320
TOKENS = 10240
ROWS = 4608
N_GROUP = 2
N_REPLICA = 16


def raised(array, key, source, target, shards_of, factor):
    def block_of(dim):
        return (jnp.arange(array.shape[dim]) // (array.shape[dim] // shards_of)).reshape((-1,) + (1,) * (array.ndim - 1 - dim))

    one_side = jax.random.permutation(key, shards_of)[block_of(target)]
    second = (block_of(target) + shards_of // 2) % shards_of
    return jnp.where((block_of(source) == one_side) | (block_of(source) == second), factor * array, array)


def block_levels(rng, extent, pieces, low, largest):
    loudness, own = 1.0, jax.random.fold_in(rng, 6)
    for dim, blocks in pieces:
        steps = jnp.exp(jax.random.uniform(jax.random.fold_in(own, dim), (blocks,), jnp.float32, low / len(pieces), largest / len(pieces)))
        loudness = loudness * jnp.repeat(steps, extent[dim] // blocks).reshape([-1 if axis == dim else 1 for axis in range(len(extent))])
    return loudness


def centred(stream_key, dims, width, reach, pieces=(), kind=jnp.bfloat16):
    loudness = block_levels(stream_key, dims, pieces, -0.22, 0.18) if pieces else 1.0
    array = jax.random.normal(stream_key, dims, jnp.float32) * width * loudness
    return jnp.minimum(jnp.maximum(array, -reach), reach).astype(kind)


def gaussian_with(key, extent, scale, bound, shards, heavy, held_as=jnp.bfloat16):
    values = scale * jax.random.normal(key, extent, jnp.float32)
    if shards:
        values = values * block_levels(key, extent, shards, -0.22, 0.18)
    return jnp.clip(raised(values, jax.random.fold_in(key, 3), *heavy), -bound, bound).astype(held_as)


def setup_inputs(seed: int = 0) -> dict:
    streams_of = jax.random.split(jax.random.key(seed), 9)
    return {
        "hidden_in": gaussian_with(streams_of[0], (TOKENS, D), 1.0, 8.0, ((0, 32),), (0, 1, 32, 2.75)),
        "w_query": centred(streams_of[1], (D, QW), D ** -0.5, 0.109375),
        "query_gain": jnp.clip(jnp.exp(jax.random.uniform(streams_of[2], (HD,), jnp.float32, math.log(0.5), math.log(2.0))), 0.5, 2.0),
        "down_projection_matrix": centred(streams_of[3], (D, R), 0.04, 0.23925781),
        "up_projection_matrix": centred(streams_of[4], (R, QW), 0.1, 0.59765625),
        "query_cotangent": gaussian_with(streams_of[5], (TOKENS, QW), 1.0, 8.0, ((0, 32),), (0, 1, 32, 2.75)),
        "first_moment": centred(streams_of[6], (ROWS, R), 0.5, 3.0, ((0, 32),), jnp.float32),
        "second_moment": jnp.clip(jnp.exp(math.log(0.1) - 4.6051702 * jax.random.uniform(streams_of[7], (ROWS, R), jnp.float32) ** block_levels(streams_of[7], (ROWS, R), ((0, 32),), -0.2, 0.2)), 0.001, 0.1),
    }


adapter_scale_factor = 0.5
norm_epsilon = 1e-06
beta_one = 0.9
beta_two = 0.999
first_bias = 1.0 - 0.9 ** 10
second_bias = 1.0 - 0.999 ** 10
learn_rate = 0.001
adam_eps = 1e-08

def queries_backward(rows_in, grads_in, w_query, query_gain, down_projection_matrix, up_projection_matrix):
    reduced_rank_input = jnp.dot(rows_in, down_projection_matrix, preferred_element_type=jnp.float32).astype(jnp.bfloat16)
    apply_projection = jnp.dot(rows_in, w_query, preferred_element_type=jnp.float32)
    apply_projection = apply_projection + adapter_scale_factor * jnp.dot(reduced_rank_input, up_projection_matrix, preferred_element_type=jnp.float32)
    token_count = apply_projection.shape[0]
    head_size = query_gain.shape[0]
    shaped = apply_projection.reshape(token_count, -1, head_size)
    inverse = lax.rsqrt(lax.optimization_barrier(jnp.mean(shaped * shaped, axis=-1, keepdims=True)) + norm_epsilon)
    normed = shaped * inverse
    upstream = grads_in.astype(jnp.float32).reshape(shaped.shape) * query_gain
    grad_pre = inverse * (upstream - normed * lax.optimization_barrier(jnp.mean(upstream * normed, axis=-1, keepdims=True)))
    grad_pre = grad_pre.reshape(token_count, -1).astype(jnp.bfloat16)
    backward_reduced = lax.dot_general(grad_pre, up_projection_matrix, (((1,), (1,)), ((), ())), preferred_element_type=jnp.float32)
    backward_reduced = (adapter_scale_factor * backward_reduced).astype(jnp.bfloat16)
    scaled_reduced = (reduced_rank_input.astype(jnp.float32) * adapter_scale_factor).astype(jnp.bfloat16)
    return (grad_pre, backward_reduced, scaled_reduced)

def adam_update(grads, params, first, second):
    first_new = beta_one * first + (1.0 - beta_one) * grads
    second_new = beta_two * second + (1.0 - beta_two) * grads * grads
    direction = first_new / first_bias / (jnp.sqrt(second_new / second_bias) + adam_eps)
    return ((params - learn_rate * direction).astype(jnp.bfloat16), first_new, second_new)

def reference(hidden_in, w_query, query_gain, down_projection_matrix, up_projection_matrix, query_cotangent, first_moment, second_moment):
    accelerator_list = N_GROUP * N_REPLICA
    rows_in = hidden_in.reshape(accelerator_list, TOK_DEV, D)
    grads_in = query_cotangent.reshape(accelerator_list, TOK_DEV, QW)

    def one_device(summed, inputs_pair):
        grad_pre, backward_reduced, scaled_reduced = queries_backward(inputs_pair[0], inputs_pair[1], w_query, query_gain, down_projection_matrix, up_projection_matrix)
        down_term = lax.dot_general(inputs_pair[0], backward_reduced, (((0,), (0,)), ((), ())), preferred_element_type=jnp.float32)
        up_term = lax.dot_general(grad_pre, scaled_reduced, (((0,), (0,)), ((), ())), preferred_element_type=jnp.float32)
        return (summed + jnp.concatenate([down_term, up_term], axis=0) / accelerator_list, None)
    grads, _ = lax.scan(one_device, jnp.zeros((D + QW, R), jnp.float32), (rows_in, grads_in))
    params = jnp.concatenate([down_projection_matrix, up_projection_matrix.T], axis=0).astype(jnp.float32)
    updated, first_new, second_new = adam_update(grads, params, first_moment, second_moment)
    return (updated[:D], updated[D:].T, first_new, second_new)
```

```python
import functools

import jax
import jax.numpy as jnp
from jax import lax
from jax.experimental import pallas as pl
from jax.experimental.pallas import tpu as pltpu
from jax.sharding import Mesh
from jax.sharding import PartitionSpec as P

adapter_scale_factor = 0.5
norm_epsilon = 1e-06
beta_one = 0.9
beta_two = 0.999
first_bias = 1.0 - 0.9**10
second_bias = 1.0 - 0.999**10
learn_rate = 0.001
adam_eps = 1e-08

LANES = 128
SUB = 8
EXTRA = 8
TOP = 14.0
TINY = 1e-30
F32 = jnp.float32
BF16 = jnp.bfloat16
EVERY = ("group", "chip", "core")
CHIPS = ("group", "chip")
SWAP = ((0, 1), (1, 0))


def lanes_of(shape):
    return lax.broadcasted_iota(jnp.int32, shape, len(shape) - 1)


def pack_tail(tile, start):
    step = LANES // SUB
    group = lanes_of((SUB, LANES)) // step
    out = None
    for r in range(SUB):
        part = tile[SUB * r : SUB * (r + 1), :]
        shift = (step * r - start) % LANES
        if not isinstance(shift, int) or shift:
            part = pltpu.roll(part, shift, 1)
        out = part if out is None else jnp.where(group == r, part, out)
    return out


def unpack_tail(tail, start):
    step = LANES // SUB
    parts = []
    for r in range(SUB):
        shift = (start - step * r) % LANES
        moved = not isinstance(shift, int) or shift
        parts.append(pltpu.roll(tail, shift, 1) if moved else tail)
    return jnp.concatenate(parts, axis=0)


def backward_kernel(
    steps,
    where_ref,
    hidden_ref,
    w_ref,
    gain_ref,
    down_ref,
    up_ref,
    cot_ref,
    *rest,
    packed,
):
    if packed:
        (first_ref, second_ref, keep_ref, send_ref, own_ref, scaled_s, back_s, grads_s, params_s) = rest
    else:
        grads_s, scaled_s, back_s = rest
    step = pl.program_id(0)
    width = w_ref.shape[1]
    head = gain_ref.shape[1]
    model_width = hidden_ref.shape[1]

    @pl.when(step == 0)
    def _():
        low = lax.dot_general(
            hidden_ref[...], down_ref[...], (((1,), (1,)), ((), ())), preferred_element_type=F32
        ).astype(BF16)
        scaled_s[...] = (low.astype(F32) * adapter_scale_factor).astype(BF16)
        back_s[...] = jnp.zeros_like(back_s)
        if packed:
            params_s[:, :model_width] = down_ref[...]

    scaled = scaled_s[...]
    up = up_ref[...]
    project = jnp.dot(hidden_ref[...], w_ref[...], preferred_element_type=F32)
    project = project + jnp.dot(scaled, up, preferred_element_type=F32)
    pieces = []
    for h in range(width // head):
        mine = project[:, h * head : (h + 1) * head]
        inverse = lax.rsqrt(jnp.mean(mine * mine, axis=-1, keepdims=True) + norm_epsilon)
        normed = mine * inverse
        upstream = cot_ref[:, h * head : (h + 1) * head].astype(F32) * gain_ref[...]
        mean = jnp.mean(upstream * normed, axis=-1, keepdims=True)
        pieces.append((inverse * (upstream - normed * mean)).astype(BF16))
    grad_pre = jnp.concatenate(pieces, axis=1)
    back_s[...] += lax.dot_general(
        grad_pre, up, (((1,), (1,)), ((), ())), preferred_element_type=F32
    )
    place = pl.ds(pl.multiple_of(model_width + step * width, LANES), width)
    grads_s[:, place] = lax.dot_general(
        scaled, grad_pre, (((0,), (0,)), ((), ())), preferred_element_type=F32
    )
    if packed:
        params_s[:, place] = up

    @pl.when(step == steps - 1)
    def _():
        back_low = (adapter_scale_factor * back_s[...]).astype(BF16)
        grads_s[:, :model_width] = lax.dot_general(
            back_low, hidden_ref[...], (((0,), (0,)), ((), ())), preferred_element_type=F32
        )
        if packed:
            pack_blocks(where_ref, grads_s, params_s, first_ref, second_ref, keep_ref, send_ref, own_ref)


def pack_blocks(where_ref, grads_s, params_s, first_ref, second_ref, keep_ref, send_ref, own_ref):
    lane = lanes_of((64, LANES))
    core = where_ref[1]
    on_zero = jnp.full((SUB, LANES), core, jnp.int32) == 0
    on_zero_main = jnp.full((64, LANES), core, jnp.int32) == 0

    def block_of(i):
        j, tile = i % SUB, i // SUB * (SUB + 1) + i % SUB
        a = grads_s[:, tile * LANES : (tile + 1) * LANES]
        b = grads_s[:, (tile + 1) * LANES : (tile + 2) * LANES]
        main = jnp.where(lane >= 16 * j, a, b) if j else a
        tail = pack_tail(b, 16 * j)
        top = jnp.maximum(jnp.max(jnp.abs(main)), jnp.max(jnp.abs(tail)))
        return main, tail, jnp.full((SUB, LANES), top, F32)

    for k in range(keep_ref.shape[0]):
        even, odd = block_of(2 * k), block_of(2 * k + 1)
        for ref, (one, two) in ((keep_ref, (even, odd)), (send_ref, (odd, even))):
            ref[k, :64] = jnp.where(on_zero_main, one[0], two[0])
            ref[k, 64:72] = jnp.where(on_zero, one[1], two[1])
            ref[k, 72:80] = jnp.where(on_zero, one[2], two[2])

    index = where_ref[0]
    j = index % SUB
    tile = index // SUB * (SUB + 1) + j
    window = params_s[:, pl.ds(pl.multiple_of(tile * LANES, LANES), 2 * LANES)].astype(F32)
    a, b = window[:, :LANES], window[:, LANES:]
    own_ref[0, :64] = jnp.where(lane >= 16 * j, a, b)
    own_ref[0, 64:72] = pack_tail(b, 16 * j)
    for n, ref in ((1, first_ref), (2, second_ref)):
        own_ref[n, :64] = pltpu.roll(ref[:, :LANES], 16 * j, 1)
        last = jnp.concatenate([ref[:, LANES:], jnp.zeros((64, LANES - 16), F32)], axis=1)
        own_ref[n, 64:72] = pack_tail(last, 0)


def finish_kernel(where_ref, mine_ref, other_ref, own_ref, down_ref, up_ref, first_ref, second_ref):
    lane = lanes_of((64, LANES))
    core = where_ref[1]
    on_zero = jnp.full((80, LANES), core, jnp.int32) == 0
    down_tiles = down_ref.shape[1] // LANES
    blocks = {}

    def block_of(i):
        if i not in blocks:
            blocks.clear()
            k = i // 2
            one, two = mine_ref[k].astype(F32), other_ref[k].astype(F32)
            blocks[2 * k] = jnp.where(on_zero, one, two)
            blocks[2 * k + 1] = jnp.where(on_zero, two, one)
        return blocks[i]

    tiles = (down_ref.shape[1] + up_ref.shape[1]) // LANES
    before = None
    for tile in range(tiles):
        group, t = tile // (SUB + 1), tile % (SUB + 1)
        value = None
        if t < SUB:
            value = block_of(SUB * group + t)
        out = value[:64] if t == 0 else None
        if t:
            out = unpack_tail(before[64:72], 16 * (t - 1))
            if t > 1:
                out = jnp.where(lane < 16 * (t - 1), before[:64], out)
            if t < SUB:
                out = jnp.where(lane >= 16 * t, value[:64], out)
        before = value
        out = out.astype(BF16)
        if tile < down_tiles:
            down_ref[:, tile * LANES : (tile + 1) * LANES] = out
        else:
            up_ref[:, (tile - down_tiles) * LANES : (tile - down_tiles + 1) * LANES] = out

    j = where_ref[0] % SUB
    for n, ref in ((0, first_ref), (1, second_ref)):
        ref[:, :LANES] = pltpu.roll(own_ref[n, :64], (LANES - 16 * j) % LANES, 1)
        ref[:, LANES:] = unpack_tail(own_ref[n, 64:72], 0)[:, :16]


def whole(shape):
    return pl.BlockSpec(shape, lambda s: (0,) * len(shape), pipeline_mode=pl.Buffered(1))


def backward(where, hidden, w_query, gain, down_t, up, cotangent, first_t, second_t, chips, packed):
    tokens, model_width = hidden.shape
    features = w_query.shape[1]
    rank = down_t.shape[0]
    head = gain.shape[1]
    width = 2 * head if features % (2 * head) == 0 else head
    steps = features // width
    rows = model_width + features
    columns = lambda n: pl.BlockSpec((n, width), lambda s: (0, s))
    in_specs = [
        pl.BlockSpec(memory_space=pltpu.SMEM),
        whole((tokens, model_width)),
        columns(model_width),
        whole((1, head)),
        whole((rank, model_width)),
        columns(rank),
        columns(tokens),
    ]
    operands = [where, hidden, w_query, gain, down_t, up, cotangent]
    scratch = [pltpu.VMEM((tokens, rank), BF16), pltpu.VMEM((tokens, rank), F32)]
    if packed:
        own = rows // chips // 2
        height = rank * own // LANES
        halves = (chips, height + EXTRA, LANES)
        in_specs += [whole((rank, own))] * 2
        operands += [first_t, second_t]
        out_shape = [jax.ShapeDtypeStruct(halves, F32)] * 2 + [
            jax.ShapeDtypeStruct((3, height, LANES), F32)
        ]
        out_specs = [whole(halves)] * 2 + [whole((3, height, LANES))]
        scratch += [pltpu.VMEM((rank, rows), F32), pltpu.VMEM((rank, rows), BF16)]
    else:
        out_shape = jax.ShapeDtypeStruct((rank, rows), F32)
        out_specs = whole((rank, rows))
    return pl.pallas_call(
        functools.partial(backward_kernel, steps, packed=packed),
        grid=(steps,),
        in_specs=in_specs,
        out_specs=out_specs,
        out_shape=out_shape,
        scratch_shapes=scratch,
        compiler_params=pltpu.CompilerParams(
            dimension_semantics=("arbitrary",), vmem_limit_bytes=48 << 20
        ),
        name="backward",
    )(*operands)


def finish(where, mine, other, own_new, model_width, features):
    rank = 64
    own = own_new.shape[1] * LANES // rank
    full = pl.BlockSpec(memory_space=pltpu.VMEM)
    return pl.pallas_call(
        finish_kernel,
        in_specs=[pl.BlockSpec(memory_space=pltpu.SMEM), full, full, full],
        out_specs=[full] * 4,
        out_shape=[
            jax.ShapeDtypeStruct((rank, model_width), BF16),
            jax.ShapeDtypeStruct((rank, features), BF16),
            jax.ShapeDtypeStruct((rank, own), F32),
            jax.ShapeDtypeStruct((rank, own), F32),
        ],
        compiler_params=pltpu.CompilerParams(vmem_limit_bytes=32 << 20),
        name="finish",
    )(where, mine, other, own_new)


def rows_of(columns):
    return columns.reshape(-1, LANES)


def on_device(
    hidden_in,
    w_query,
    query_gain,
    down_projection_matrix,
    up_projection_matrix,
    query_cotangent,
    first_moment,
    second_moment,
):
    model_width, rank = down_projection_matrix.shape
    features = up_projection_matrix.shape[1]
    chips = lax.axis_size(CHIPS)
    devices = 2 * chips
    own = (model_width + features) // devices
    height = rank * own // LANES
    packed = rank == 64 and own == LANES + 16 and model_width % LANES == 0 and chips % 4 == 0
    core = lax.axis_index("core")
    index = lax.axis_index(EVERY)
    where = jnp.stack([index, core]).astype(jnp.int32)
    down_t = down_projection_matrix.T
    result = backward(
        where,
        hidden_in,
        w_query,
        query_gain[None, :],
        down_t,
        up_projection_matrix,
        query_cotangent,
        first_moment.T,
        second_moment.T,
        chips,
        packed,
    )
    if packed:
        keep, send, own_state = result
        params, first, second = own_state[0], own_state[1], own_state[2]
    else:
        blocks = result.reshape(rank, chips, 2, own).transpose(2, 1, 0, 3).reshape(2, chips, height, LANES)
        top = jnp.max(jnp.abs(blocks), axis=(2, 3), keepdims=True)
        blocks = jnp.concatenate([blocks, jnp.broadcast_to(top, (2, chips, EXTRA, LANES))], axis=2)
        keep = lax.dynamic_index_in_dim(blocks, core, 0, keepdims=False)
        send = lax.dynamic_index_in_dim(blocks, 1 - core, 0, keepdims=False)
        combined = jnp.concatenate([down_t, up_projection_matrix], axis=1)
        params = rows_of(lax.dynamic_slice_in_dim(combined, index * own, own, 1)).astype(F32)
        first, second = rows_of(first_moment.T), rows_of(second_moment.T)

    other = lax.ppermute(send, "core", SWAP)
    total = keep + other
    bound = jnp.maximum(keep[:, height : height + 1] + other[:, height : height + 1], TINY)
    power = jnp.ceil(jnp.log2(bound)) - TOP
    is_value = lax.broadcasted_iota(jnp.int32, total.shape, 1) < height
    coded = jnp.where(is_value, total * jnp.exp2(-power), power).astype(jnp.float16)
    arrived = lax.all_to_all(coded, CHIPS, 0, 0, tiled=True)

    grads = None
    for k in range(chips):
        power = arrived[k, height : height + 1].astype(F32)
        term = arrived[k, :height].astype(F32) * jnp.exp2(power)
        grads = term if grads is None else grads + term
    grads = grads / devices
    first_new = beta_one * first + (1.0 - beta_one) * grads
    second_new = beta_two * second + (1.0 - beta_two) * grads * grads
    direction = first_new / first_bias / (jnp.sqrt(second_new / second_bias) + adam_eps)
    updated = (params - learn_rate * direction).astype(BF16)

    updated = jnp.pad(updated, ((0, EXTRA), (0, 0)))
    copies = jnp.broadcast_to(updated[None], (chips, height + EXTRA, LANES))
    mine = lax.all_to_all(copies, CHIPS, 0, 0, tiled=True)
    other = lax.ppermute(mine, "core", SWAP)
    if packed:
        own_new = jnp.stack([first_new, second_new])
        down_new, up_new, first_out, second_out = finish(where, mine, other, own_new, model_width, features)
    else:
        pair = jnp.stack([mine, other])
        pair = jnp.where(core == 0, pair, pair[::-1])[:, :, :height]
        columns = pair.reshape(2, chips, rank, own).transpose(2, 1, 0, 3).reshape(rank, devices * own)
        down_new, up_new = columns[:, :model_width], columns[:, model_width:]
        first_out, second_out = first_new.reshape(rank, own), second_new.reshape(rank, own)
    return (down_new.T, up_new, first_out.T, second_out.T)


def solution(mesh):
    groups, replicas = mesh.shape["group"], mesh.shape["replica"]
    fine = Mesh(mesh.devices.reshape(groups, replicas // 2, 2), EVERY)
    rows = P(EVERY, None)
    return jax.shard_map(
        on_device,
        mesh=fine,
        in_specs=(rows, P(), P(), P(), P(), rows, rows, rows),
        out_specs=(P(), P(), rows, rows),
        check_vma=False,
    )
```

```python
import functools

import jax
import jax.numpy as jnp
from jax import lax
from jax.experimental import pallas as pl
from jax.experimental.pallas import tpu as pltpu
from jax.sharding import Mesh
from jax.sharding import PartitionSpec as P

adapter_scale_factor = 0.5
norm_epsilon = 1e-06
beta_one = 0.9
beta_two = 0.999
first_bias = 1.0 - 0.9**10
second_bias = 1.0 - 0.999**10
learn_rate = 0.001
adam_eps = 1e-08

LANES = 128
SUB = 8
EXTRA = 8
TOP = 14.0
TINY = 1e-30
F32 = jnp.float32
BF16 = jnp.bfloat16
EVERY = ("group", "chip", "core")
CHIPS = ("group", "chip")
SWAP = ((0, 1), (1, 0))


def lanes_of(shape):
    return lax.broadcasted_iota(jnp.int32, shape, len(shape) - 1)


def pack_tail(tile, start):
    step = LANES // SUB
    group = lanes_of((SUB, LANES)) // step
    out = None
    for r in range(SUB):
        part = tile[SUB * r : SUB * (r + 1), :]
        shift = (step * r - start) % LANES
        if not isinstance(shift, int) or shift:
            part = pltpu.roll(part, shift, 1)
        out = part if out is None else jnp.where(group == r, part, out)
    return out


def unpack_tail(tail, start):
    step = LANES // SUB
    parts = []
    for r in range(SUB):
        shift = (start - step * r) % LANES
        moved = not isinstance(shift, int) or shift
        parts.append(pltpu.roll(tail, shift, 1) if moved else tail)
    return jnp.concatenate(parts, axis=0)


def backward_kernel(steps, *refs, packed):
    if packed:
        (where_ref, hidden_h, w_h, gain_h, down_h, up_h, cot_h, first_h, second_h) = refs[:9]
        (keep_ref, send_ref, own_ref) = refs[9:12]
        (hidden, w, gain, down, up, cot, project_s, grads_s, first_s, second_s, sems) = refs[12:]
    else:
        (where_ref, hidden_h, w_h, gain_h, down_h, up_h, cot_h) = refs[:7]
        grads_s = refs[7]
        (hidden, w, gain, down, up, cot, project_s, sems) = refs[8:]
    tokens, model_width = hidden.shape
    width = w.shape[2]
    head = gain.shape[1]
    features = up.shape[1]
    copies = {}

    def fetch(name, source, target):
        copy = pltpu.make_async_copy(source, target, sems.at[len(copies)])
        copy.start()
        copies[name] = copy

    fetch("hidden", hidden_h, hidden)
    fetch("down", down_h, down)
    for j in range(steps):
        place = pl.ds(j * width, width)
        fetch(("w", j), w_h.at[:, place], w.at[j])
        if j == 0:
            fetch("up", up_h, up)
            fetch("gain", gain_h, gain)
        fetch(("cot", j), cot_h.at[:, place], cot.at[j])
    if packed:
        fetch("first", first_h, first_s)
        fetch("second", second_h, second_s)

    copies["hidden"].wait()
    copies["down"].wait()
    low = lax.dot_general(
        hidden[...], down[...], (((1,), (1,)), ((), ())), preferred_element_type=F32
    ).astype(BF16)
    scaled = (low.astype(F32) * adapter_scale_factor).astype(BF16)
    back = jnp.zeros(scaled.shape, F32)
    done = 0
    for j in range(steps + 1):
        if j < steps:
            copies["w", j].wait()
            project_s[j % 2] = jnp.dot(hidden[...], w[j], preferred_element_type=F32)
        if j == 0:
            copies["up"].wait()
            copies["gain"].wait()
            continue
        copies["cot", j - 1].wait()
        up_part = up[:, (j - 1) * width : j * width]
        project = project_s[(j - 1) % 2] + jnp.dot(scaled, up_part, preferred_element_type=F32)
        pieces = []
        for h in range(width // head):
            mine = project[:, h * head : (h + 1) * head]
            inverse = lax.rsqrt(jnp.mean(mine * mine, axis=-1, keepdims=True) + norm_epsilon)
            normed = mine * inverse
            upstream = cot[j - 1, :, h * head : (h + 1) * head].astype(F32) * gain[...]
            mean = jnp.mean(upstream * normed, axis=-1, keepdims=True)
            pieces.append((inverse * (upstream - normed * mean)).astype(BF16))
        grad_pre = jnp.concatenate(pieces, axis=1)
        back = back + lax.dot_general(
            grad_pre, up_part, (((1,), (1,)), ((), ())), preferred_element_type=F32
        )
        place = slice(model_width + (j - 1) * width, model_width + j * width)
        grads_s[:, place] = lax.dot_general(
            scaled, grad_pre, (((0,), (0,)), ((), ())), preferred_element_type=F32
        )

    back_low = (adapter_scale_factor * back).astype(BF16)
    part = 6 * LANES if model_width % (6 * LANES) == 0 else model_width
    for start in range(0, model_width, part):
        grads_s[:, start : start + part] = lax.dot_general(
            back_low,
            hidden[:, start : start + part],
            (((0,), (0,)), ((), ())),
            preferred_element_type=F32,
        )
    if packed:
        copies["first"].wait()
        copies["second"].wait()
        pack_blocks(where_ref, grads_s, down, up, first_s, second_s, keep_ref, send_ref, own_ref)


def pack_blocks(where_ref, grads_s, down, up, first_s, second_s, keep_ref, send_ref, own_ref):
    lane = lanes_of((64, LANES))
    core = where_ref[1]
    on_zero = jnp.full((SUB, LANES), core, jnp.int32) == 0
    on_zero_main = jnp.full((64, LANES), core, jnp.int32) == 0

    def block_of(i):
        j, tile = i % SUB, i // SUB * (SUB + 1) + i % SUB
        a = grads_s[:, tile * LANES : (tile + 1) * LANES]
        b = grads_s[:, (tile + 1) * LANES : (tile + 2) * LANES]
        main = jnp.where(lane >= 16 * j, a, b) if j else a
        tail = pack_tail(b, 16 * j)
        top = jnp.abs(tail)
        for r in range(SUB):
            top = jnp.maximum(top, jnp.abs(main[SUB * r : SUB * (r + 1)]))
        return main, tail, top

    for k in range(keep_ref.shape[0]):
        even, odd = block_of(2 * k), block_of(2 * k + 1)
        for ref, (one, two) in ((keep_ref, (even, odd)), (send_ref, (odd, even))):
            ref[k, :64] = jnp.where(on_zero_main, one[0], two[0])
            ref[k, 64:72] = jnp.where(on_zero, one[1], two[1])
            ref[k, 72:80] = jnp.where(on_zero, one[2], two[2])

    index = where_ref[0]
    j = index % SUB
    tile = index // SUB * (SUB + 1) + j
    tiles = down.shape[1] // LANES

    def params_at(t):
        t_down = jnp.minimum(t, tiles - 1)
        t_up = jnp.maximum(t - tiles, 0)
        a = down[:, pl.ds(pl.multiple_of(t_down * LANES, LANES), LANES)].astype(F32)
        b = up[:, pl.ds(pl.multiple_of(t_up * LANES, LANES), LANES)].astype(F32)
        return jnp.where(jnp.full((64, LANES), t, jnp.int32) < tiles, a, b)

    a, b = params_at(tile), params_at(tile + 1)
    own_ref[0, :64] = jnp.where(lane >= 16 * j, a, b)
    own_ref[0, 64:72] = pack_tail(b, 16 * j)
    for n, ref in ((1, first_s), (2, second_s)):
        own_ref[n, :64] = pltpu.roll(ref[:, :LANES], 16 * j, 1)
        last = jnp.concatenate([ref[:, LANES:], jnp.zeros((64, LANES - 16), F32)], axis=1)
        own_ref[n, 64:72] = pack_tail(last, 0)


def finish_kernel(where_ref, mine_ref, other_ref, own_ref, down_ref, up_ref, first_ref, second_ref):
    lane = lanes_of((64, LANES))
    core = where_ref[1]
    on_zero = jnp.full((72, LANES), core, jnp.int32) == 0
    down_tiles = down_ref.shape[1] // LANES
    blocks = {}

    def block_of(i):
        if i not in blocks:
            blocks.clear()
            k = i // 2
            one, two = mine_ref[k].astype(F32), other_ref[k].astype(F32)
            blocks[2 * k] = jnp.where(on_zero, one, two)
            blocks[2 * k + 1] = jnp.where(on_zero, two, one)
        return blocks[i]

    tiles = (down_ref.shape[1] + up_ref.shape[1]) // LANES
    before = None
    for tile in range(tiles):
        group, t = tile // (SUB + 1), tile % (SUB + 1)
        value = None
        if t < SUB:
            value = block_of(SUB * group + t)
        out = value[:64] if t == 0 else None
        if t:
            out = unpack_tail(before[64:72], 16 * (t - 1))
            if t > 1:
                out = jnp.where(lane < 16 * (t - 1), before[:64], out)
            if t < SUB:
                out = jnp.where(lane >= 16 * t, value[:64], out)
        before = value
        out = out.astype(BF16)
        if tile < down_tiles:
            down_ref[:, tile * LANES : (tile + 1) * LANES] = out
        else:
            up_ref[:, (tile - down_tiles) * LANES : (tile - down_tiles + 1) * LANES] = out

    j = where_ref[0] % SUB
    for n, ref in ((0, first_ref), (1, second_ref)):
        ref[:, :LANES] = pltpu.roll(own_ref[n, :64], (LANES - 16 * j) % LANES, 1)
        ref[:, LANES:] = unpack_tail(own_ref[n, 64:72], 0)[:, :16]


def backward(where, hidden, w_query, gain, down_t, up, cotangent, first_t, second_t, chips, packed):
    tokens, model_width = hidden.shape
    features = w_query.shape[1]
    rank = down_t.shape[0]
    head = gain.shape[1]
    width = 2 * head if features % (2 * head) == 0 else head
    steps = features // width
    rows = model_width + features
    far = pl.BlockSpec(memory_space=pltpu.HBM)
    near = pl.BlockSpec(memory_space=pltpu.VMEM)
    operands = [hidden, w_query, gain, down_t, up, cotangent]
    scratch = [
        pltpu.VMEM((tokens, model_width), BF16),
        pltpu.VMEM((steps, model_width, width), BF16),
        pltpu.VMEM((1, head), F32),
        pltpu.VMEM((rank, model_width), BF16),
        pltpu.VMEM((rank, features), BF16),
        pltpu.VMEM((steps, tokens, width), BF16),
        pltpu.VMEM((2, tokens, width), F32),
    ]
    if packed:
        own = rows // chips // 2
        height = rank * own // LANES
        halves = (chips, height + EXTRA, LANES)
        operands += [first_t, second_t]
        out_shape = [jax.ShapeDtypeStruct(halves, F32)] * 2 + [
            jax.ShapeDtypeStruct((3, height, LANES), F32)
        ]
        out_specs = [near] * 3
        scratch += [pltpu.VMEM((rank, rows), F32)] + [pltpu.VMEM((rank, own), F32)] * 2
    else:
        out_shape = jax.ShapeDtypeStruct((rank, rows), F32)
        out_specs = near
    scratch += [pltpu.SemaphoreType.DMA((2 * steps + 6,))]
    operands = [pltpu.with_memory_space_constraint(x, pltpu.HBM) for x in operands]
    return pl.pallas_call(
        functools.partial(backward_kernel, steps, packed=packed),
        in_specs=[pl.BlockSpec(memory_space=pltpu.SMEM)] + [far] * len(operands),
        out_specs=out_specs,
        out_shape=out_shape,
        scratch_shapes=scratch,
        compiler_params=pltpu.CompilerParams(vmem_limit_bytes=32 << 20),
        name="backward",
    )(where, *operands)


def finish(where, mine, other, own_new, model_width, features):
    rank = 64
    own = own_new.shape[1] * LANES // rank
    full = pl.BlockSpec(memory_space=pltpu.VMEM)
    return pl.pallas_call(
        finish_kernel,
        in_specs=[pl.BlockSpec(memory_space=pltpu.SMEM), full, full, full],
        out_specs=[full] * 4,
        out_shape=[
            jax.ShapeDtypeStruct((rank, model_width), BF16),
            jax.ShapeDtypeStruct((rank, features), BF16),
            jax.ShapeDtypeStruct((rank, own), F32),
            jax.ShapeDtypeStruct((rank, own), F32),
        ],
        compiler_params=pltpu.CompilerParams(vmem_limit_bytes=32 << 20),
        name="finish",
    )(where, mine, other, own_new)


def rows_of(columns):
    return columns.reshape(-1, LANES)


def on_device(
    hidden_in,
    w_query,
    query_gain,
    down_projection_matrix,
    up_projection_matrix,
    query_cotangent,
    first_moment,
    second_moment,
):
    model_width, rank = down_projection_matrix.shape
    features = up_projection_matrix.shape[1]
    chips = lax.axis_size(CHIPS)
    devices = 2 * chips
    own = (model_width + features) // devices
    height = rank * own // LANES
    groups = -(-height // SUB)
    packed = rank == 64 and own == LANES + 16 and model_width % LANES == 0 and chips % 4 == 0
    core = lax.axis_index("core")
    index = lax.axis_index(EVERY)
    where = jnp.stack([index, core]).astype(jnp.int32)
    down_t = down_projection_matrix.T
    result = backward(
        where,
        hidden_in,
        w_query,
        query_gain[None, :],
        down_t,
        up_projection_matrix,
        query_cotangent,
        first_moment.T,
        second_moment.T,
        chips,
        packed,
    )
    if packed:
        keep, send, own_state = result
        params, first, second = own_state[0], own_state[1], own_state[2]
    else:
        blocks = result.reshape(rank, chips, 2, own).transpose(2, 1, 0, 3).reshape(2, chips, -1, LANES)
        blocks = jnp.pad(blocks, ((0, 0), (0, 0), (0, groups * SUB - height), (0, 0)))
        top = jnp.max(jnp.abs(blocks).reshape(2, chips, groups, SUB, LANES), axis=2)
        blocks = jnp.concatenate([blocks, top], axis=2)
        keep = lax.dynamic_index_in_dim(blocks, core, 0, keepdims=False)
        send = lax.dynamic_index_in_dim(blocks, 1 - core, 0, keepdims=False)
        combined = jnp.concatenate([down_t, up_projection_matrix], axis=1)
        params = rows_of(lax.dynamic_slice_in_dim(combined, index * own, own, 1)).astype(F32)
        first, second = rows_of(first_moment.T), rows_of(second_moment.T)

    total = (keep + lax.ppermute(send, "core", SWAP)).reshape(chips, groups + 1, SUB, LANES)
    power = jnp.ceil(jnp.log2(jnp.maximum(total[:, groups:], TINY))) - TOP
    is_value = lax.broadcasted_iota(jnp.int32, total.shape, 1) < groups
    coded = jnp.where(is_value, total * jnp.exp2(-power), power).astype(jnp.float16)
    arrived = lax.all_to_all(coded, CHIPS, 0, 0, tiled=True)

    grads = None
    for k in range(chips):
        term = arrived[k, :groups].astype(F32) * jnp.exp2(arrived[k, groups:].astype(F32))
        grads = term if grads is None else grads + term
    grads = grads.reshape(groups * SUB, LANES)[:height]
    grads = grads / devices
    first_new = beta_one * first + (1.0 - beta_one) * grads
    second_new = beta_two * second + (1.0 - beta_two) * grads * grads
    direction = first_new / first_bias / (jnp.sqrt(second_new / second_bias) + adam_eps)
    updated = (params - learn_rate * direction).astype(BF16)

    copies = jnp.broadcast_to(updated[None], (chips, height, LANES))
    copies, first_new, second_new = lax.optimization_barrier((copies, first_new, second_new))
    mine = lax.all_to_all(copies, CHIPS, 0, 0, tiled=True)
    other = lax.ppermute(mine, "core", SWAP)
    if packed:
        own_new = jnp.stack([first_new, second_new])
        down_new, up_new, first_out, second_out = finish(where, mine, other, own_new, model_width, features)
    else:
        pair = jnp.stack([mine, other])
        pair = jnp.where(core == 0, pair, pair[::-1])
        columns = pair.reshape(2, chips, rank, own).transpose(2, 1, 0, 3).reshape(rank, devices * own)
        down_new, up_new = columns[:, :model_width], columns[:, model_width:]
        first_out, second_out = first_new.reshape(rank, own), second_new.reshape(rank, own)
    return (down_new.T, up_new, first_out.T, second_out.T)


def solution(mesh):
    groups, replicas = mesh.shape["group"], mesh.shape["replica"]
    fine = Mesh(mesh.devices.reshape(groups, replicas // 2, 2), EVERY)
    rows = P(EVERY, None)
    return jax.shard_map(
        on_device,
        mesh=fine,
        in_specs=(rows, P(), P(), P(), P(), rows, rows, rows),
        out_specs=(P(), P(), rows, rows),
        check_vma=False,
    )
```

```python
import functools

import jax
import jax.numpy as jnp
from jax import lax
from jax.experimental import pallas as pl
from jax.experimental.pallas import tpu as pltpu
from jax.sharding import Mesh
from jax.sharding import PartitionSpec as P

adapter_scale_factor = 0.5
norm_epsilon = 1e-06
beta_one = 0.9
beta_two = 0.999
first_bias = 1.0 - 0.9**10
second_bias = 1.0 - 0.999**10
learn_rate = 0.001
adam_eps = 1e-08

LANES = 128
SUB = 8
EXTRA = 8
TOP = 14.0
TINY = 1e-30
PIECES = 2
F32 = jnp.float32
BF16 = jnp.bfloat16
EVERY = ("group", "chip", "core")
CHIPS = ("group", "chip")
SWAP = ((0, 1), (1, 0))


def lanes_of(shape):
    return lax.broadcasted_iota(jnp.int32, shape, len(shape) - 1)


def pack_tail(tile, start):
    step = LANES // SUB
    group = lanes_of((SUB, LANES)) // step
    out = None
    for r in range(SUB):
        part = tile[SUB * r : SUB * (r + 1), :]
        shift = (step * r - start) % LANES
        if not isinstance(shift, int) or shift:
            part = pltpu.roll(part, shift, 1)
        out = part if out is None else jnp.where(group == r, part, out)
    return out


def unpack_tail(tail, start):
    step = LANES // SUB
    parts = []
    for r in range(SUB):
        shift = (start - step * r) % LANES
        moved = not isinstance(shift, int) or shift
        parts.append(pltpu.roll(tail, shift, 1) if moved else tail)
    return jnp.concatenate(parts, axis=0)


def backward_kernel(steps, *refs, packed):
    if packed:
        (where_ref, hidden_h, w_h, gain_h, down_h, up_h, cot_h, first_h, second_h) = refs[:9]
        (keep_ref, send_ref, own_ref) = refs[9:12]
        (hidden, w, gain, down, up, cot, project_s, grad_s, back_s, turned, grads_s, first_s, second_s, sems) = refs[12:]
    else:
        (where_ref, hidden_h, w_h, gain_h, down_h, up_h, cot_h) = refs[:7]
        grads_s = refs[7]
        (hidden, w, gain, down, up, cot, project_s, grad_s, back_s, turned, sems) = refs[8:]
    tokens, model_width = hidden_h.shape
    width = w.shape[2]
    head = gain.shape[1]
    rank, features = up.shape
    full = model_width + rank
    piece = model_width // PIECES

    def block(ref, j):
        return ref.at[:, pl.ds(pl.multiple_of(j * width, width), width)]

    def part(ref, i):
        return ref.at[:, pl.ds(pl.multiple_of(i * piece, piece), piece)]

    def hidden_copy(i):
        return pltpu.make_async_copy(part(hidden_h, i), part(hidden, i), sems.at[i])

    def w_copy(j):
        return pltpu.make_async_copy(block(w_h, j), w.at[j, :model_width], sems.at[PIECES + j])

    def up_copy(j):
        return pltpu.make_async_copy(
            block(up_h, j), w.at[j, model_width:full], sems.at[PIECES + steps + j]
        )

    def cot_copy(j):
        return pltpu.make_async_copy(block(cot_h, j), cot.at[j], sems.at[PIECES + 2 * steps + j])

    single = [(down_h, down), (gain_h, gain), (up_h, up)]
    if packed:
        single += [(first_h, first_s), (second_h, second_s)]
    single = [
        pltpu.make_async_copy(source, target, sems.at[PIECES + 3 * steps + n])
        for n, (source, target) in enumerate(single)
    ]

    def each(n, body):
        lax.fori_loop(0, n, lambda i, _: body(i), None)

    single[0].start()
    each(PIECES, lambda i: hidden_copy(i).start())
    single[1].start()

    def start_block(j):
        up_copy(j).start()
        cot_copy(j).start()
        w_copy(j).start()

    each(steps, start_block)
    for copy in single[2:]:
        copy.start()

    back_s[...] = jnp.zeros_like(back_s)
    single[0].wait()

    def add_low(i):
        hidden_copy(i).wait()
        back_s[...] += lax.dot_general(
            part(hidden, i)[...],
            part(down, i)[...],
            (((1,), (1,)), ((), ())),
            preferred_element_type=F32,
        )

    each(PIECES, add_low)
    low = back_s[...].astype(BF16)
    scaled = (low.astype(F32) * adapter_scale_factor).astype(BF16)
    hidden[:, model_width:] = scaled
    turned[...] = scaled.T
    single[1].wait()

    def normalise(j):
        for h in range(width // head):
            place = slice(h * head, (h + 1) * head)
            mine = project_s[:, place]
            upstream = cot[j, :, place].astype(F32) * gain[...]
            inverse = lax.rsqrt(jnp.mean(mine * mine, axis=-1, keepdims=True) + norm_epsilon)
            normed = mine * inverse
            mean = jnp.mean(upstream * normed, axis=-1, keepdims=True)
            place = pl.ds(pl.multiple_of(j * width + h * head, head), head)
            grad_s[:, place] = (inverse * (upstream - normed * mean)).astype(BF16)

    def step(j, _):
        w_copy(j).wait()
        up_copy(j).wait()
        cot_copy(j).wait()
        before = jnp.maximum(j - 1, 0)
        normalise(before)
        project_s[...] = jnp.dot(hidden[...], w[j], preferred_element_type=F32)

    project_s[...] = jnp.zeros_like(project_s)
    lax.fori_loop(0, steps, step, None)
    normalise(steps - 1)
    single[2].wait()
    back = lax.dot_general(
        grad_s[...], up[...], (((1,), (1,)), ((), ())), preferred_element_type=F32
    )
    back_low = (adapter_scale_factor * back).astype(BF16).T
    grads_s[:, model_width:] = jnp.dot(turned[...], grad_s[...], preferred_element_type=F32)
    grads_s[:, :model_width] = jnp.dot(
        back_low, hidden[:, :model_width], preferred_element_type=F32
    )
    if packed:
        for copy in single[3:]:
            copy.wait()
        pack_blocks(where_ref, grads_s, down, up, first_s, second_s, keep_ref, send_ref, own_ref)


def pack_blocks(where_ref, grads_s, down, up, first_s, second_s, keep_ref, send_ref, own_ref):
    lane = lanes_of((64, LANES))
    core = where_ref[1]
    on_zero = jnp.full((SUB, LANES), core, jnp.int32) == 0
    on_zero_main = jnp.full((64, LANES), core, jnp.int32) == 0

    def tile_of(t):
        return grads_s[:, pl.ds(pl.multiple_of(t * LANES, LANES), LANES)]

    def block_of(group, j):
        a, b = tile_of(group * (SUB + 1) + j), tile_of(group * (SUB + 1) + j + 1)
        main = jnp.where(lane >= 16 * j, a, b) if j else a
        tail = pack_tail(b, 16 * j)
        top = jnp.abs(tail)
        for r in range(SUB):
            top = jnp.maximum(top, jnp.abs(main[SUB * r : SUB * (r + 1)]))
        return main, tail, top

    def pack_group(group, _):
        for k in range(SUB // 2):
            even, odd = block_of(group, 2 * k), block_of(group, 2 * k + 1)
            chip = group * (SUB // 2) + k
            for ref, (one, two) in ((keep_ref, (even, odd)), (send_ref, (odd, even))):
                ref[chip, :64] = jnp.where(on_zero_main, one[0], two[0])
                ref[chip, 64:72] = jnp.where(on_zero, one[1], two[1])
                ref[chip, 72:80] = jnp.where(on_zero, one[2], two[2])

    lax.fori_loop(0, keep_ref.shape[0] // (SUB // 2), pack_group, None)

    index = where_ref[0]
    j = index % SUB
    tile = index // SUB * (SUB + 1) + j
    tiles = down.shape[1] // LANES

    def params_at(t):
        t_down = jnp.minimum(t, tiles - 1)
        t_up = jnp.maximum(t - tiles, 0)
        a = down[:, pl.ds(pl.multiple_of(t_down * LANES, LANES), LANES)].astype(F32)
        b = up[:, pl.ds(pl.multiple_of(t_up * LANES, LANES), LANES)].astype(F32)
        return jnp.where(jnp.full((64, LANES), t, jnp.int32) < tiles, a, b)

    a, b = params_at(tile), params_at(tile + 1)
    own_ref[0, :64] = jnp.where(lane >= 16 * j, a, b)
    own_ref[0, 64:72] = pack_tail(b, 16 * j)
    for n, ref in ((1, first_s), (2, second_s)):
        own_ref[n, :64] = pltpu.roll(ref[:, :LANES], 16 * j, 1)
        last = jnp.concatenate([ref[:, LANES:], jnp.zeros((64, LANES - 16), F32)], axis=1)
        own_ref[n, 64:72] = pack_tail(last, 0)


def finish_kernel(where_ref, mine_ref, other_ref, own_ref, down_ref, up_ref, first_ref, second_ref):
    lane = lanes_of((64, LANES))
    core = where_ref[1]
    on_zero = jnp.full((72, LANES), core, jnp.int32) == 0
    down_tiles = down_ref.shape[1] // LANES
    blocks = {}

    def block_of(i):
        if i not in blocks:
            blocks.clear()
            k = i // 2
            one, two = mine_ref[k].astype(F32), other_ref[k].astype(F32)
            blocks[2 * k] = jnp.where(on_zero, one, two)
            blocks[2 * k + 1] = jnp.where(on_zero, two, one)
        return blocks[i]

    tiles = (down_ref.shape[1] + up_ref.shape[1]) // LANES
    before = None
    for tile in range(tiles):
        group, t = tile // (SUB + 1), tile % (SUB + 1)
        value = None
        if t < SUB:
            value = block_of(SUB * group + t)
        out = value[:64] if t == 0 else None
        if t:
            out = unpack_tail(before[64:72], 16 * (t - 1))
            if t > 1:
                out = jnp.where(lane < 16 * (t - 1), before[:64], out)
            if t < SUB:
                out = jnp.where(lane >= 16 * t, value[:64], out)
        before = value
        out = out.astype(BF16)
        if tile < down_tiles:
            down_ref[:, tile * LANES : (tile + 1) * LANES] = out
        else:
            up_ref[:, (tile - down_tiles) * LANES : (tile - down_tiles + 1) * LANES] = out

    j = where_ref[0] % SUB
    for n, ref in ((0, first_ref), (1, second_ref)):
        ref[:, :LANES] = pltpu.roll(own_ref[n, :64], (LANES - 16 * j) % LANES, 1)
        ref[:, LANES:] = unpack_tail(own_ref[n, 64:72], 0)[:, :16]


def backward(where, hidden, w_query, gain, down_t, up, cotangent, first_t, second_t, chips, packed):
    tokens, model_width = hidden.shape
    features = w_query.shape[1]
    rank = down_t.shape[0]
    head = gain.shape[1]
    width = 2 * head if features % (2 * head) == 0 else head
    steps = features // width
    rows = model_width + features
    depth = model_width + rank
    far = pl.BlockSpec(memory_space=pltpu.HBM)
    near = pl.BlockSpec(memory_space=pltpu.VMEM)
    operands = [hidden, w_query, gain, down_t, up, cotangent]
    scratch = [
        pltpu.VMEM((tokens, depth), BF16),
        pltpu.VMEM((steps, depth, width), BF16),
        pltpu.VMEM((1, head), F32),
        pltpu.VMEM((rank, model_width), BF16),
        pltpu.VMEM((rank, features), BF16),
        pltpu.VMEM((steps, tokens, width), BF16),
        pltpu.VMEM((tokens, width), F32),
        pltpu.VMEM((tokens, features), BF16),
        pltpu.VMEM((tokens, rank), F32),
        pltpu.VMEM((rank, tokens), BF16),
    ]
    if packed:
        own = rows // chips // 2
        height = rank * own // LANES
        halves = (chips, height + EXTRA, LANES)
        operands += [first_t, second_t]
        out_shape = [jax.ShapeDtypeStruct(halves, F32)] * 2 + [
            jax.ShapeDtypeStruct((3, height, LANES), F32)
        ]
        out_specs = [near] * 3
        scratch += [pltpu.VMEM((rank, rows), F32)] + [pltpu.VMEM((rank, own), F32)] * 2
    else:
        out_shape = jax.ShapeDtypeStruct((rank, rows), F32)
        out_specs = near
    scratch += [pltpu.SemaphoreType.DMA((3 * steps + PIECES + 5,))]
    operands = [pltpu.with_memory_space_constraint(x, pltpu.HBM) for x in operands]
    return pl.pallas_call(
        functools.partial(backward_kernel, steps, packed=packed),
        in_specs=[pl.BlockSpec(memory_space=pltpu.SMEM)] + [far] * len(operands),
        out_specs=out_specs,
        out_shape=out_shape,
        scratch_shapes=scratch,
        compiler_params=pltpu.CompilerParams(vmem_limit_bytes=32 << 20),
        name="backward",
    )(where, *operands)


def finish(where, mine, other, own_new, model_width, features):
    rank = 64
    own = own_new.shape[1] * LANES // rank
    full = pl.BlockSpec(memory_space=pltpu.VMEM)
    return pl.pallas_call(
        finish_kernel,
        in_specs=[pl.BlockSpec(memory_space=pltpu.SMEM), full, full, full],
        out_specs=[full] * 4,
        out_shape=[
            jax.ShapeDtypeStruct((rank, model_width), BF16),
            jax.ShapeDtypeStruct((rank, features), BF16),
            jax.ShapeDtypeStruct((rank, own), F32),
            jax.ShapeDtypeStruct((rank, own), F32),
        ],
        compiler_params=pltpu.CompilerParams(vmem_limit_bytes=32 << 20),
        name="finish",
    )(where, mine, other, own_new)


def rows_of(columns):
    return columns.reshape(-1, LANES)


def on_device(
    hidden_in,
    w_query,
    query_gain,
    down_projection_matrix,
    up_projection_matrix,
    query_cotangent,
    first_moment,
    second_moment,
):
    model_width, rank = down_projection_matrix.shape
    features = up_projection_matrix.shape[1]
    chips = lax.axis_size(CHIPS)
    devices = 2 * chips
    own = (model_width + features) // devices
    height = rank * own // LANES
    groups = -(-height // SUB)
    packed = rank == 64 and own == LANES + 16 and model_width % LANES == 0 and chips % 4 == 0
    core = lax.axis_index("core")
    index = lax.axis_index(EVERY)
    where = jnp.stack([index, core]).astype(jnp.int32)
    down_t = down_projection_matrix.T
    result = backward(
        where,
        hidden_in,
        w_query,
        query_gain[None, :],
        down_t,
        up_projection_matrix,
        query_cotangent,
        first_moment.T,
        second_moment.T,
        chips,
        packed,
    )
    if packed:
        keep, send, own_state = result
        params, first, second = own_state[0], own_state[1], own_state[2]
    else:
        blocks = result.reshape(rank, chips, 2, own).transpose(2, 1, 0, 3).reshape(2, chips, -1, LANES)
        blocks = jnp.pad(blocks, ((0, 0), (0, 0), (0, groups * SUB - height), (0, 0)))
        top = jnp.max(jnp.abs(blocks).reshape(2, chips, groups, SUB, LANES), axis=2)
        blocks = jnp.concatenate([blocks, top], axis=2)
        keep = lax.dynamic_index_in_dim(blocks, core, 0, keepdims=False)
        send = lax.dynamic_index_in_dim(blocks, 1 - core, 0, keepdims=False)
        combined = jnp.concatenate([down_t, up_projection_matrix], axis=1)
        params = rows_of(lax.dynamic_slice_in_dim(combined, index * own, own, 1)).astype(F32)
        first, second = rows_of(first_moment.T), rows_of(second_moment.T)

    total = (keep + lax.ppermute(send, "core", SWAP)).reshape(chips, groups + 1, SUB, LANES)
    power = jnp.ceil(jnp.log2(jnp.maximum(total[:, groups:], TINY))) - TOP
    is_value = lax.broadcasted_iota(jnp.int32, total.shape, 1) < groups
    coded = jnp.where(is_value, total * jnp.exp2(-power), power).astype(jnp.float16)
    arrived = lax.all_to_all(coded, CHIPS, 0, 0, tiled=True)

    grads = None
    for k in range(chips):
        term = arrived[k, :groups].astype(F32) * jnp.exp2(arrived[k, groups:].astype(F32))
        grads = term if grads is None else grads + term
    grads = grads.reshape(groups * SUB, LANES)[:height]
    grads = grads / devices
    first_new = beta_one * first + (1.0 - beta_one) * grads
    second_new = beta_two * second + (1.0 - beta_two) * grads * grads
    direction = first_new / first_bias / (jnp.sqrt(second_new / second_bias) + adam_eps)
    updated = (params - learn_rate * direction).astype(BF16)

    copies = jnp.broadcast_to(updated[None], (chips, height, LANES))
    copies, first_new, second_new = lax.optimization_barrier((copies, first_new, second_new))
    mine = lax.all_to_all(copies, CHIPS, 0, 0, tiled=True)
    other = lax.ppermute(mine, "core", SWAP)
    if packed:
        own_new = jnp.stack([first_new, second_new])
        down_new, up_new, first_out, second_out = finish(where, mine, other, own_new, model_width, features)
    else:
        pair = jnp.stack([mine, other])
        pair = jnp.where(core == 0, pair, pair[::-1])
        columns = pair.reshape(2, chips, rank, own).transpose(2, 1, 0, 3).reshape(rank, devices * own)
        down_new, up_new = columns[:, :model_width], columns[:, model_width:]
        first_out, second_out = first_new.reshape(rank, own), second_new.reshape(rank, own)
    return (down_new.T, up_new, first_out.T, second_out.T)


def solution(mesh):
    groups, replicas = mesh.shape["group"], mesh.shape["replica"]
    fine = Mesh(mesh.devices.reshape(groups, replicas // 2, 2), EVERY)
    rows = P(EVERY, None)
    return jax.shard_map(
        on_device,
        mesh=fine,
        in_specs=(rows, P(), P(), P(), P(), rows, rows, rows),
        out_specs=(P(), P(), rows, rows),
        check_vma=False,
    )
```

```python
import functools

import jax
import jax.numpy as jnp
from jax import lax
from jax.experimental import pallas as pl
from jax.experimental.pallas import tpu as pltpu
from jax.sharding import Mesh
from jax.sharding import PartitionSpec as P

adapter_scale_factor = 0.5
norm_epsilon = 1e-06
beta_one = 0.9
beta_two = 0.999
first_bias = 1.0 - 0.9**10
second_bias = 1.0 - 0.999**10
learn_rate = 0.001
adam_eps = 1e-08

LANES = 128
SUB = 8
RANGE = 2.0**-11
PIECES = 2
F32 = jnp.float32
BF16 = jnp.bfloat16
EVERY = ("group", "chip", "core")
CHIPS = ("group", "chip")
SWAP = ((0, 1), (1, 0))


def lanes_of(shape):
    return lax.broadcasted_iota(jnp.int32, shape, len(shape) - 1)


def pack_tail(tile, start):
    step = LANES // SUB
    group = lanes_of((SUB, LANES)) // step
    out = None
    for r in range(SUB):
        part = tile[SUB * r : SUB * (r + 1), :]
        shift = (step * r - start) % LANES
        if not isinstance(shift, int) or shift:
            part = pltpu.roll(part, shift, 1)
        out = part if out is None else jnp.where(group == r, part, out)
    return out


def unpack_tail(tail, start):
    step = LANES // SUB
    parts = []
    for r in range(SUB):
        shift = (start - step * r) % LANES
        moved = not isinstance(shift, int) or shift
        parts.append(pltpu.roll(tail, shift, 1) if moved else tail)
    return jnp.concatenate(parts, axis=0)


def backward_kernel(steps, *refs, packed):
    if packed:
        (where_ref, hidden_h, w_h, gain_h, down_h, up_h, cot_h, first_h, second_h) = refs[:9]
        (keep_ref, send_ref, own_ref) = refs[9:12]
        (hidden, w, gain, down, up, cot, project_s, grad_s, back_s, turned, grads_s, first_s, second_s, sems) = refs[12:]
    else:
        (where_ref, hidden_h, w_h, gain_h, down_h, up_h, cot_h) = refs[:7]
        grads_s = refs[7]
        (hidden, w, gain, down, up, cot, project_s, grad_s, back_s, turned, sems) = refs[8:]
    tokens, model_width = hidden_h.shape
    width = w.shape[2]
    head = gain.shape[1]
    rank, features = up.shape
    full = model_width + rank
    piece = model_width // PIECES

    def block(ref, j):
        return ref.at[:, pl.ds(pl.multiple_of(j * width, width), width)]

    def part(ref, i):
        return ref.at[:, pl.ds(pl.multiple_of(i * piece, piece), piece)]

    def hidden_copy(i):
        return pltpu.make_async_copy(part(hidden_h, i), part(hidden, i), sems.at[i])

    def w_copy(j):
        return pltpu.make_async_copy(block(w_h, j), w.at[j, :model_width], sems.at[PIECES + j])

    def up_copy(j):
        return pltpu.make_async_copy(
            block(up_h, j), w.at[j, model_width:full], sems.at[PIECES + steps + j]
        )

    def cot_copy(j):
        return pltpu.make_async_copy(block(cot_h, j), cot.at[j], sems.at[PIECES + 2 * steps + j])

    single = [(down_h, down), (gain_h, gain), (up_h, up)]
    if packed:
        single += [(first_h, first_s), (second_h, second_s)]
    single = [
        pltpu.make_async_copy(source, target, sems.at[PIECES + 3 * steps + n])
        for n, (source, target) in enumerate(single)
    ]

    def each(n, body):
        lax.fori_loop(0, n, lambda i, _: body(i), None)

    single[0].start()
    each(PIECES, lambda i: hidden_copy(i).start())
    single[1].start()

    def start_block(j):
        up_copy(j).start()
        cot_copy(j).start()
        w_copy(j).start()

    each(steps, start_block)
    for copy in single[2:]:
        copy.start()

    back_s[...] = jnp.zeros_like(back_s)
    single[0].wait()

    def add_low(i):
        hidden_copy(i).wait()
        back_s[...] += lax.dot_general(
            part(hidden, i)[...],
            part(down, i)[...],
            (((1,), (1,)), ((), ())),
            preferred_element_type=F32,
        )

    each(PIECES, add_low)
    low = back_s[...].astype(BF16)
    scaled = (low.astype(F32) * adapter_scale_factor).astype(BF16)
    hidden[:, model_width:] = scaled
    turned[...] = scaled.T
    single[1].wait()

    def normalise(j):
        for h in range(width // head):
            place = slice(h * head, (h + 1) * head)
            mine = project_s[:, place]
            upstream = cot[j, :, place].astype(F32) * gain[...]
            inverse = lax.rsqrt(jnp.mean(mine * mine, axis=-1, keepdims=True) + norm_epsilon)
            normed = mine * inverse
            mean = jnp.mean(upstream * normed, axis=-1, keepdims=True)
            place = pl.ds(pl.multiple_of(j * width + h * head, head), head)
            grad_s[:, place] = (inverse * (upstream - normed * mean)).astype(BF16)

    def step(j, _):
        w_copy(j).wait()
        up_copy(j).wait()
        cot_copy(j).wait()
        before = jnp.maximum(j - 1, 0)
        normalise(before)
        project_s[...] = jnp.dot(hidden[...], w[j], preferred_element_type=F32)

    project_s[...] = jnp.zeros_like(project_s)
    lax.fori_loop(0, steps, step, None)
    single[2].wait()
    normalise(steps - 1)
    done = model_width + features - width
    grads_s[:, model_width:done] = jnp.dot(
        turned[...], grad_s[:, : features - width], preferred_element_type=F32
    )
    back = lax.dot_general(
        grad_s[...], up[...], (((1,), (1,)), ((), ())), preferred_element_type=F32
    )
    back_low = (adapter_scale_factor * back).astype(BF16).T
    grads_s[:, done:] = jnp.dot(
        turned[...], grad_s[:, features - width :], preferred_element_type=F32
    )
    grads_s[:, :model_width] = jnp.dot(
        back_low, hidden[:, :model_width], preferred_element_type=F32
    )
    if packed:
        for copy in single[3:]:
            copy.wait()
        pack_blocks(where_ref, grads_s, down, up, first_s, second_s, keep_ref, send_ref, own_ref)


def pack_blocks(where_ref, grads_s, down, up, first_s, second_s, keep_ref, send_ref, own_ref):
    lane = lanes_of((64, LANES))
    core = where_ref[1]
    on_zero = jnp.full((SUB, LANES), core, jnp.int32) == 0
    on_zero_main = jnp.full((64, LANES), core, jnp.int32) == 0

    def tile_of(t):
        return grads_s[:, t * LANES : (t + 1) * LANES]

    def block_of(group, j):
        a, b = tile_of(group * (SUB + 1) + j), tile_of(group * (SUB + 1) + j + 1)
        main = jnp.where(lane >= 16 * j, a, b) if j else a
        return main, pack_tail(b, 16 * j)

    def pack_group(group):
        for k in range(SUB // 2):
            even, odd = block_of(group, 2 * k), block_of(group, 2 * k + 1)
            chip = group * (SUB // 2) + k
            for ref, (one, two) in ((keep_ref, (even, odd)), (send_ref, (odd, even))):
                ref[chip, :64] = jnp.where(on_zero_main, one[0], two[0])
                ref[chip, 64:72] = jnp.where(on_zero, one[1], two[1])

    for group in reversed(range(keep_ref.shape[0] // (SUB // 2))):
        pack_group(group)

    index = where_ref[0]
    j = index % SUB
    tile = index // SUB * (SUB + 1) + j
    tiles = down.shape[1] // LANES

    def params_at(t):
        t_down = jnp.minimum(t, tiles - 1)
        t_up = jnp.maximum(t - tiles, 0)
        a = down[:, pl.ds(pl.multiple_of(t_down * LANES, LANES), LANES)].astype(F32)
        b = up[:, pl.ds(pl.multiple_of(t_up * LANES, LANES), LANES)].astype(F32)
        return jnp.where(jnp.full((64, LANES), t, jnp.int32) < tiles, a, b)

    a, b = params_at(tile), params_at(tile + 1)
    own_ref[0, :64] = jnp.where(lane >= 16 * j, a, b)
    own_ref[0, 64:72] = pack_tail(b, 16 * j)
    for n, ref in ((1, first_s), (2, second_s)):
        own_ref[n, :64] = pltpu.roll(ref[:, :LANES], 16 * j, 1)
        last = jnp.concatenate([ref[:, LANES:], jnp.zeros((64, LANES - 16), F32)], axis=1)
        own_ref[n, 64:72] = pack_tail(last, 0)


def finish_kernel(where_ref, mine_ref, other_ref, own_ref, down_ref, up_ref, first_ref, second_ref):
    lane = lanes_of((64, LANES))
    core = where_ref[1]
    on_zero = jnp.full((72, LANES), core, jnp.int32) == 0
    down_tiles = down_ref.shape[1] // LANES
    blocks = {}

    def block_of(i):
        if i not in blocks:
            blocks.clear()
            k = i // 2
            one, two = mine_ref[k].astype(F32), other_ref[k].astype(F32)
            blocks[2 * k] = jnp.where(on_zero, one, two)
            blocks[2 * k + 1] = jnp.where(on_zero, two, one)
        return blocks[i]

    tiles = (down_ref.shape[1] + up_ref.shape[1]) // LANES
    before = None
    for tile in range(tiles):
        group, t = tile // (SUB + 1), tile % (SUB + 1)
        value = None
        if t < SUB:
            value = block_of(SUB * group + t)
        out = value[:64] if t == 0 else None
        if t:
            out = unpack_tail(before[64:72], 16 * (t - 1))
            if t > 1:
                out = jnp.where(lane < 16 * (t - 1), before[:64], out)
            if t < SUB:
                out = jnp.where(lane >= 16 * t, value[:64], out)
        before = value
        out = out.astype(BF16)
        if tile < down_tiles:
            down_ref[:, tile * LANES : (tile + 1) * LANES] = out
        else:
            up_ref[:, (tile - down_tiles) * LANES : (tile - down_tiles + 1) * LANES] = out

    j = where_ref[0] % SUB
    for n, ref in ((0, first_ref), (1, second_ref)):
        ref[:, :LANES] = pltpu.roll(own_ref[n, :64], (LANES - 16 * j) % LANES, 1)
        ref[:, LANES:] = unpack_tail(own_ref[n, 64:72], 0)[:, :16]


def backward(where, hidden, w_query, gain, down_t, up, cotangent, first_t, second_t, chips, packed):
    tokens, model_width = hidden.shape
    features = w_query.shape[1]
    rank = down_t.shape[0]
    head = gain.shape[1]
    width = 2 * head if features % (2 * head) == 0 else head
    steps = features // width
    rows = model_width + features
    depth = model_width + rank
    far = pl.BlockSpec(memory_space=pltpu.HBM)
    near = pl.BlockSpec(memory_space=pltpu.VMEM)
    operands = [hidden, w_query, gain, down_t, up, cotangent]
    scratch = [
        pltpu.VMEM((tokens, depth), BF16),
        pltpu.VMEM((steps, depth, width), BF16),
        pltpu.VMEM((1, head), F32),
        pltpu.VMEM((rank, model_width), BF16),
        pltpu.VMEM((rank, features), BF16),
        pltpu.VMEM((steps, tokens, width), BF16),
        pltpu.VMEM((tokens, width), F32),
        pltpu.VMEM((tokens, features), BF16),
        pltpu.VMEM((tokens, rank), F32),
        pltpu.VMEM((rank, tokens), BF16),
    ]
    if packed:
        own = rows // chips // 2
        height = rank * own // LANES
        halves = (chips, height, LANES)
        operands += [first_t, second_t]
        out_shape = [jax.ShapeDtypeStruct(halves, F32)] * 2 + [
            jax.ShapeDtypeStruct((3, height, LANES), F32)
        ]
        out_specs = [near] * 3
        scratch += [pltpu.VMEM((rank, rows), F32)] + [pltpu.VMEM((rank, own), F32)] * 2
    else:
        out_shape = jax.ShapeDtypeStruct((rank, rows), F32)
        out_specs = near
    scratch += [pltpu.SemaphoreType.DMA((3 * steps + PIECES + 5,))]
    operands = [pltpu.with_memory_space_constraint(x, pltpu.HBM) for x in operands]
    return pl.pallas_call(
        functools.partial(backward_kernel, steps, packed=packed),
        in_specs=[pl.BlockSpec(memory_space=pltpu.SMEM)] + [far] * len(operands),
        out_specs=out_specs,
        out_shape=out_shape,
        scratch_shapes=scratch,
        compiler_params=pltpu.CompilerParams(vmem_limit_bytes=32 << 20),
        name="backward",
    )(where, *operands)


def finish(where, mine, other, own_new, model_width, features):
    rank = 64
    own = own_new.shape[1] * LANES // rank
    full = pl.BlockSpec(memory_space=pltpu.VMEM)
    return pl.pallas_call(
        finish_kernel,
        in_specs=[pl.BlockSpec(memory_space=pltpu.SMEM), full, full, full],
        out_specs=[full] * 4,
        out_shape=[
            jax.ShapeDtypeStruct((rank, model_width), BF16),
            jax.ShapeDtypeStruct((rank, features), BF16),
            jax.ShapeDtypeStruct((rank, own), F32),
            jax.ShapeDtypeStruct((rank, own), F32),
        ],
        compiler_params=pltpu.CompilerParams(vmem_limit_bytes=32 << 20),
        name="finish",
    )(where, mine, other, own_new)


def coded_of(g):
    root = jnp.sqrt(jnp.abs(g) * RANGE)
    return jnp.where(g < 0, -root, root).astype(jnp.float16)


def decoded_of(code):
    root = code.astype(F32)
    return root * jnp.abs(root)


def rows_of(columns):
    return columns.reshape(-1, LANES)


def on_device(
    hidden_in,
    w_query,
    query_gain,
    down_projection_matrix,
    up_projection_matrix,
    query_cotangent,
    first_moment,
    second_moment,
):
    model_width, rank = down_projection_matrix.shape
    features = up_projection_matrix.shape[1]
    chips = lax.axis_size(CHIPS)
    devices = 2 * chips
    own = (model_width + features) // devices
    height = rank * own // LANES
    packed = rank == 64 and own == LANES + 16 and model_width % LANES == 0 and chips % 4 == 0
    core = lax.axis_index("core")
    index = lax.axis_index(EVERY)
    where = jnp.stack([index, core]).astype(jnp.int32)
    down_t = down_projection_matrix.T
    result = backward(
        where,
        hidden_in,
        w_query,
        query_gain[None, :],
        down_t,
        up_projection_matrix,
        query_cotangent,
        first_moment.T,
        second_moment.T,
        chips,
        packed,
    )
    if packed:
        keep, send, own_state = result
        params, first, second = own_state[0], own_state[1], own_state[2]
    else:
        blocks = result.reshape(rank, chips, 2, own).transpose(2, 1, 0, 3).reshape(2, chips, -1, LANES)
        keep = lax.dynamic_index_in_dim(blocks, core, 0, keepdims=False)
        send = lax.dynamic_index_in_dim(blocks, 1 - core, 0, keepdims=False)
        combined = jnp.concatenate([down_t, up_projection_matrix], axis=1)
        params = rows_of(lax.dynamic_slice_in_dim(combined, index * own, own, 1)).astype(F32)
        first, second = rows_of(first_moment.T), rows_of(second_moment.T)

    coded = coded_of(keep + lax.ppermute(send, "core", SWAP))
    arrived = lax.all_to_all(coded, CHIPS, 0, 0, tiled=True)
    grads = None
    for k in range(chips):
        term = decoded_of(arrived[k])
        grads = term if grads is None else grads + term
    grads = grads / (RANGE * devices)
    first_new = beta_one * first + (1.0 - beta_one) * grads
    second_new = beta_two * second + (1.0 - beta_two) * grads * grads
    direction = first_new / first_bias / (jnp.sqrt(second_new / second_bias) + adam_eps)
    updated = (params - learn_rate * direction).astype(BF16)

    copies = jnp.broadcast_to(updated[None], (chips, height, LANES))
    copies, first_new, second_new = lax.optimization_barrier((copies, first_new, second_new))
    mine = lax.all_to_all(copies, CHIPS, 0, 0, tiled=True)
    other = lax.ppermute(mine, "core", SWAP)
    if packed:
        own_new = jnp.stack([first_new, second_new])
        down_new, up_new, first_out, second_out = finish(where, mine, other, own_new, model_width, features)
    else:
        pair = jnp.stack([mine, other])
        pair = jnp.where(core == 0, pair, pair[::-1])
        columns = pair.reshape(2, chips, rank, own).transpose(2, 1, 0, 3).reshape(rank, devices * own)
        down_new, up_new = columns[:, :model_width], columns[:, model_width:]
        first_out, second_out = first_new.reshape(rank, own), second_new.reshape(rank, own)
    return (down_new.T, up_new, first_out.T, second_out.T)


def solution(mesh):
    groups, replicas = mesh.shape["group"], mesh.shape["replica"]
    fine = Mesh(mesh.devices.reshape(groups, replicas // 2, 2), EVERY)
    rows = P(EVERY, None)
    return jax.shard_map(
        on_device,
        mesh=fine,
        in_specs=(rows, P(), P(), P(), P(), rows, rows, rows),
        out_specs=(P(), P(), rows, rows),
        check_vma=False,
    )
```

```python
import functools

import jax
import jax.numpy as jnp
from jax import lax
from jax.experimental import pallas as pl
from jax.experimental.pallas import tpu as pltpu
from jax.sharding import Mesh
from jax.sharding import PartitionSpec as P

adapter_scale_factor = 0.5
norm_epsilon = 1e-06
beta_one = 0.9
beta_two = 0.999
first_bias = 1.0 - 0.9**10
second_bias = 1.0 - 0.999**10
learn_rate = 0.001
adam_eps = 1e-08

LANES = 128
SUB = 8
RANGE = 2.0**-11
PIECES = 2
F32 = jnp.float32
BF16 = jnp.bfloat16
EVERY = ("group", "chip", "core")
CHIPS = ("group", "chip")
SWAP = ((0, 1), (1, 0))


def lanes_of(shape):
    return lax.broadcasted_iota(jnp.int32, shape, len(shape) - 1)


def pack_tail(tile, start):
    step = LANES // SUB
    group = lanes_of((SUB, LANES)) // step
    out = None
    for r in range(SUB):
        part = tile[SUB * r : SUB * (r + 1), :]
        shift = (step * r - start) % LANES
        if not isinstance(shift, int) or shift:
            part = pltpu.roll(part, shift, 1)
        out = part if out is None else jnp.where(group == r, part, out)
    return out


def unpack_tail(tail, start):
    step = LANES // SUB
    parts = []
    for r in range(SUB):
        shift = (start - step * r) % LANES
        moved = not isinstance(shift, int) or shift
        parts.append(pltpu.roll(tail, shift, 1) if moved else tail)
    return jnp.concatenate(parts, axis=0)


def backward_kernel(steps, *refs, packed):
    if packed:
        (where_ref, hidden_h, w_h, gain_h, down_h, up_h, cot_h, first_h, second_h) = refs[:9]
        (keep_ref, send_ref, own_ref) = refs[9:12]
        (hidden, w, gain, down, up, cot, project_s, grad_s, back_s, turned, grads_s, first_s, second_s, sems) = refs[12:]
    else:
        (where_ref, hidden_h, w_h, gain_h, down_h, up_h, cot_h) = refs[:7]
        grads_s = refs[7]
        (hidden, w, gain, down, up, cot, project_s, grad_s, back_s, turned, sems) = refs[8:]
    tokens, model_width = hidden_h.shape
    width = w.shape[2]
    head = gain.shape[1]
    rank, features = up.shape
    full = model_width + rank
    piece = model_width // PIECES

    def block(ref, j):
        return ref.at[:, pl.ds(pl.multiple_of(j * width, width), width)]

    def part(ref, i):
        return ref.at[:, pl.ds(pl.multiple_of(i * piece, piece), piece)]

    def hidden_copy(i):
        return pltpu.make_async_copy(part(hidden_h, i), part(hidden, i), sems.at[i])

    def w_copy(j):
        return pltpu.make_async_copy(block(w_h, j), w.at[j, :model_width], sems.at[PIECES + j])

    def up_copy(j):
        return pltpu.make_async_copy(
            block(up_h, j), w.at[j, model_width:full], sems.at[PIECES + steps + j]
        )

    def cot_copy(j):
        return pltpu.make_async_copy(block(cot_h, j), cot.at[j], sems.at[PIECES + 2 * steps + j])

    single = [(down_h, down), (gain_h, gain), (up_h, up)]
    if packed:
        single += [(first_h, first_s), (second_h, second_s)]
    single = [
        pltpu.make_async_copy(source, target, sems.at[PIECES + 3 * steps + n])
        for n, (source, target) in enumerate(single)
    ]

    def each(n, body):
        lax.fori_loop(0, n, lambda i, _: body(i), None)

    single[0].start()
    each(PIECES, lambda i: hidden_copy(i).start())
    single[1].start()

    def start_block(j):
        up_copy(j).start()
        cot_copy(j).start()
        w_copy(j).start()

    each(steps, start_block)
    for copy in single[2:]:
        copy.start()

    back_s[...] = jnp.zeros_like(back_s)
    single[0].wait()

    def add_low(i):
        hidden_copy(i).wait()
        back_s[...] += lax.dot_general(
            part(hidden, i)[...],
            part(down, i)[...],
            (((1,), (1,)), ((), ())),
            preferred_element_type=F32,
        )

    each(PIECES, add_low)
    low = back_s[...].astype(BF16)
    scaled = (low.astype(F32) * adapter_scale_factor).astype(BF16)
    hidden[:, model_width:] = scaled
    turned[...] = scaled.T
    single[1].wait()

    def normalise(j):
        for h in range(width // head):
            place = slice(h * head, (h + 1) * head)
            mine = project_s[:, place]
            upstream = cot[j, :, place].astype(F32) * gain[...]
            inverse = lax.rsqrt(jnp.mean(mine * mine, axis=-1, keepdims=True) + norm_epsilon)
            normed = mine * inverse
            mean = jnp.mean(upstream * normed, axis=-1, keepdims=True)
            place = pl.ds(pl.multiple_of(j * width + h * head, head), head)
            grad_s[:, place] = (inverse * (upstream - normed * mean)).astype(BF16)

    def step(j, _):
        w_copy(j).wait()
        up_copy(j).wait()
        cot_copy(j).wait()
        before = jnp.maximum(j - 1, 0)
        normalise(before)
        project_s[...] = jnp.dot(hidden[...], w[j], preferred_element_type=F32)

    project_s[...] = jnp.zeros_like(project_s)
    lax.fori_loop(0, steps, step, None)
    single[2].wait()
    normalise(steps - 1)
    done = model_width + features - width
    grads_s[:, model_width:done] = jnp.dot(
        turned[...], grad_s[:, : features - width], preferred_element_type=F32
    )
    back = lax.dot_general(
        grad_s[...], up[...], (((1,), (1,)), ((), ())), preferred_element_type=F32
    )
    back_low = (adapter_scale_factor * back).astype(BF16).T
    grads_s[:, done:] = jnp.dot(
        turned[...], grad_s[:, features - width :], preferred_element_type=F32
    )
    turned[...] = back_low
    half = model_width // 2

    def down_half(i):
        place = pl.ds(pl.multiple_of(i * half, half), half)
        grads_s[:, place] = jnp.dot(turned[...], hidden[:, place], preferred_element_type=F32)

    each(2, down_half)
    if packed:
        for copy in single[3:]:
            copy.wait()
        pack_blocks(where_ref, grads_s, down, up, first_s, second_s, keep_ref, send_ref, own_ref)


def pack_blocks(where_ref, grads_s, down, up, first_s, second_s, keep_ref, send_ref, own_ref):
    lane = lanes_of((64, LANES))
    core = where_ref[1]
    on_zero = jnp.full((SUB, LANES), core, jnp.int32) == 0
    on_zero_main = jnp.full((64, LANES), core, jnp.int32) == 0

    def tile_of(t):
        return grads_s[:, t * LANES : (t + 1) * LANES]

    def block_of(group, j):
        a, b = tile_of(group * (SUB + 1) + j), tile_of(group * (SUB + 1) + j + 1)
        main = jnp.where(lane >= 16 * j, a, b) if j else a
        return main, pack_tail(b, 16 * j)

    def pack_group(group):
        for k in range(SUB // 2):
            even, odd = block_of(group, 2 * k), block_of(group, 2 * k + 1)
            chip = group * (SUB // 2) + k
            for ref, (one, two) in ((keep_ref, (even, odd)), (send_ref, (odd, even))):
                ref[chip, :64] = jnp.where(on_zero_main, one[0], two[0])
                ref[chip, 64:72] = jnp.where(on_zero, one[1], two[1])

    for group in reversed(range(keep_ref.shape[0] // (SUB // 2))):
        pack_group(group)

    index = where_ref[0]
    j = index % SUB
    tile = index // SUB * (SUB + 1) + j
    tiles = down.shape[1] // LANES

    def params_at(t):
        t_down = jnp.minimum(t, tiles - 1)
        t_up = jnp.maximum(t - tiles, 0)
        a = down[:, pl.ds(pl.multiple_of(t_down * LANES, LANES), LANES)].astype(F32)
        b = up[:, pl.ds(pl.multiple_of(t_up * LANES, LANES), LANES)].astype(F32)
        return jnp.where(jnp.full((64, LANES), t, jnp.int32) < tiles, a, b)

    a, b = params_at(tile), params_at(tile + 1)
    own_ref[0, :64] = jnp.where(lane >= 16 * j, a, b)
    own_ref[0, 64:72] = pack_tail(b, 16 * j)
    for n, ref in ((1, first_s), (2, second_s)):
        own_ref[n, :64] = pltpu.roll(ref[:, :LANES], 16 * j, 1)
        last = jnp.concatenate([ref[:, LANES:], jnp.zeros((64, LANES - 16), F32)], axis=1)
        own_ref[n, 64:72] = pack_tail(last, 0)


def finish_kernel(where_ref, mine_ref, other_ref, own_ref, down_ref, up_ref, first_ref, second_ref):
    lane = lanes_of((64, LANES))
    core = where_ref[1]
    on_zero = jnp.full((72, LANES), core, jnp.int32) == 0
    down_tiles = down_ref.shape[1] // LANES
    blocks = {}

    def block_of(i):
        if i not in blocks:
            blocks.clear()
            k = i // 2
            one, two = mine_ref[k].astype(F32), other_ref[k].astype(F32)
            blocks[2 * k] = jnp.where(on_zero, one, two)
            blocks[2 * k + 1] = jnp.where(on_zero, two, one)
        return blocks[i]

    tiles = (down_ref.shape[1] + up_ref.shape[1]) // LANES
    before = None
    for tile in range(tiles):
        group, t = tile // (SUB + 1), tile % (SUB + 1)
        value = None
        if t < SUB:
            value = block_of(SUB * group + t)
        out = value[:64] if t == 0 else None
        if t:
            out = unpack_tail(before[64:72], 16 * (t - 1))
            if t > 1:
                out = jnp.where(lane < 16 * (t - 1), before[:64], out)
            if t < SUB:
                out = jnp.where(lane >= 16 * t, value[:64], out)
        before = value
        out = out.astype(BF16)
        if tile < down_tiles:
            down_ref[:, tile * LANES : (tile + 1) * LANES] = out
        else:
            up_ref[:, (tile - down_tiles) * LANES : (tile - down_tiles + 1) * LANES] = out

    j = where_ref[0] % SUB
    for n, ref in ((0, first_ref), (1, second_ref)):
        ref[:, :LANES] = pltpu.roll(own_ref[n, :64], (LANES - 16 * j) % LANES, 1)
        ref[:, LANES:] = unpack_tail(own_ref[n, 64:72], 0)[:, :16]


def backward(where, hidden, w_query, gain, down_t, up, cotangent, first_t, second_t, chips, packed):
    tokens, model_width = hidden.shape
    features = w_query.shape[1]
    rank = down_t.shape[0]
    head = gain.shape[1]
    width = 2 * head if features % (2 * head) == 0 else head
    steps = features // width
    rows = model_width + features
    depth = model_width + rank
    far = pl.BlockSpec(memory_space=pltpu.HBM)
    near = pl.BlockSpec(memory_space=pltpu.VMEM)
    operands = [hidden, w_query, gain, down_t, up, cotangent]
    scratch = [
        pltpu.VMEM((tokens, depth), BF16),
        pltpu.VMEM((steps, depth, width), BF16),
        pltpu.VMEM((1, head), F32),
        pltpu.VMEM((rank, model_width), BF16),
        pltpu.VMEM((rank, features), BF16),
        pltpu.VMEM((steps, tokens, width), BF16),
        pltpu.VMEM((tokens, width), F32),
        pltpu.VMEM((tokens, features), BF16),
        pltpu.VMEM((tokens, rank), F32),
        pltpu.VMEM((rank, tokens), BF16),
    ]
    if packed:
        own = rows // chips // 2
        height = rank * own // LANES
        halves = (chips, height, LANES)
        operands += [first_t, second_t]
        out_shape = [jax.ShapeDtypeStruct(halves, F32)] * 2 + [
            jax.ShapeDtypeStruct((3, height, LANES), F32)
        ]
        out_specs = [near] * 3
        scratch += [pltpu.VMEM((rank, rows), F32)] + [pltpu.VMEM((rank, own), F32)] * 2
    else:
        out_shape = jax.ShapeDtypeStruct((rank, rows), F32)
        out_specs = near
    scratch += [pltpu.SemaphoreType.DMA((3 * steps + PIECES + 5,))]
    operands = [pltpu.with_memory_space_constraint(x, pltpu.HBM) for x in operands]
    return pl.pallas_call(
        functools.partial(backward_kernel, steps, packed=packed),
        in_specs=[pl.BlockSpec(memory_space=pltpu.SMEM)] + [far] * len(operands),
        out_specs=out_specs,
        out_shape=out_shape,
        scratch_shapes=scratch,
        compiler_params=pltpu.CompilerParams(vmem_limit_bytes=32 << 20),
        name="backward",
    )(where, *operands)


def finish(where, mine, other, own_new, model_width, features):
    rank = 64
    own = own_new.shape[1] * LANES // rank
    full = pl.BlockSpec(memory_space=pltpu.VMEM)
    return pl.pallas_call(
        finish_kernel,
        in_specs=[pl.BlockSpec(memory_space=pltpu.SMEM), full, full, full],
        out_specs=[full] * 4,
        out_shape=[
            jax.ShapeDtypeStruct((rank, model_width), BF16),
            jax.ShapeDtypeStruct((rank, features), BF16),
            jax.ShapeDtypeStruct((rank, own), F32),
            jax.ShapeDtypeStruct((rank, own), F32),
        ],
        compiler_params=pltpu.CompilerParams(vmem_limit_bytes=32 << 20),
        name="finish",
    )(where, mine, other, own_new)


def coded_of(g):
    root = jnp.sqrt(jnp.abs(g) * RANGE)
    return jnp.where(g < 0, -root, root).astype(jnp.float16)


def decoded_of(code):
    root = code.astype(F32)
    return root * jnp.abs(root)


def rows_of(columns):
    return columns.reshape(-1, LANES)


def on_device(
    hidden_in,
    w_query,
    query_gain,
    down_projection_matrix,
    up_projection_matrix,
    query_cotangent,
    first_moment,
    second_moment,
):
    model_width, rank = down_projection_matrix.shape
    features = up_projection_matrix.shape[1]
    chips = lax.axis_size(CHIPS)
    devices = 2 * chips
    own = (model_width + features) // devices
    height = rank * own // LANES
    packed = rank == 64 and own == LANES + 16 and model_width % LANES == 0 and chips % 4 == 0
    core = lax.axis_index("core")
    index = lax.axis_index(EVERY)
    where = jnp.stack([index, core]).astype(jnp.int32)
    down_t = down_projection_matrix.T
    result = backward(
        where,
        hidden_in,
        w_query,
        query_gain[None, :],
        down_t,
        up_projection_matrix,
        query_cotangent,
        first_moment.T,
        second_moment.T,
        chips,
        packed,
    )
    if packed:
        keep, send, own_state = result
        params, first, second = own_state[0], own_state[1], own_state[2]
    else:
        blocks = result.reshape(rank, chips, 2, own).transpose(2, 1, 0, 3).reshape(2, chips, -1, LANES)
        keep = lax.dynamic_index_in_dim(blocks, core, 0, keepdims=False)
        send = lax.dynamic_index_in_dim(blocks, 1 - core, 0, keepdims=False)
        combined = jnp.concatenate([down_t, up_projection_matrix], axis=1)
        params = rows_of(lax.dynamic_slice_in_dim(combined, index * own, own, 1)).astype(F32)
        first, second = rows_of(first_moment.T), rows_of(second_moment.T)

    coded = coded_of(keep + lax.ppermute(send, "core", SWAP))
    arrived = lax.all_to_all(coded, CHIPS, 0, 0, tiled=True)
    grads = None
    for k in range(chips):
        term = decoded_of(arrived[k])
        grads = term if grads is None else grads + term
    grads = grads / (RANGE * devices)
    first_new = beta_one * first + (1.0 - beta_one) * grads
    second_new = beta_two * second + (1.0 - beta_two) * grads * grads
    direction = first_new / first_bias / (jnp.sqrt(second_new / second_bias) + adam_eps)
    updated = (params - learn_rate * direction).astype(BF16)

    copies = jnp.broadcast_to(updated[None], (chips, height, LANES))
    copies, first_new, second_new = lax.optimization_barrier((copies, first_new, second_new))
    mine = lax.all_to_all(copies, CHIPS, 0, 0, tiled=True)
    other = lax.ppermute(mine, "core", SWAP)
    if packed:
        own_new = jnp.stack([first_new, second_new])
        down_new, up_new, first_out, second_out = finish(where, mine, other, own_new, model_width, features)
    else:
        pair = jnp.stack([mine, other])
        pair = jnp.where(core == 0, pair, pair[::-1])
        columns = pair.reshape(2, chips, rank, own).transpose(2, 1, 0, 3).reshape(rank, devices * own)
        down_new, up_new = columns[:, :model_width], columns[:, model_width:]
        first_out, second_out = first_new.reshape(rank, own), second_new.reshape(rank, own)
    return (down_new.T, up_new, first_out.T, second_out.T)


def solution(mesh):
    groups, replicas = mesh.shape["group"], mesh.shape["replica"]
    fine = Mesh(mesh.devices.reshape(groups, replicas // 2, 2), EVERY)
    rows = P(EVERY, None)
    return jax.shard_map(
        on_device,
        mesh=fine,
        in_specs=(rows, P(), P(), P(), P(), rows, rows, rows),
        out_specs=(P(), P(), rows, rows),
        check_vma=False,
    )
```

```python
import functools

import jax
import jax.numpy as jnp
from jax import lax
from jax.experimental import pallas as pl
from jax.experimental.pallas import tpu as pltpu
from jax.sharding import Mesh
from jax.sharding import PartitionSpec as P

adapter_scale_factor = 0.5
norm_epsilon = 1e-06
beta_one = 0.9
beta_two = 0.999
first_bias = 1.0 - 0.9**10
second_bias = 1.0 - 0.999**10
learn_rate = 0.001
adam_eps = 1e-08

LANES = 128
SUB = 8
RANGE = 2.0**-11
TINY = 2.0**-100
PIECES = 2
F32 = jnp.float32
BF16 = jnp.bfloat16
EVERY = ("group", "chip", "core")
CHIPS = ("group", "chip")
SWAP = ((0, 1), (1, 0))


def lanes_of(shape):
    return lax.broadcasted_iota(jnp.int32, shape, len(shape) - 1)


def pack_tail(tile, start):
    step = LANES // SUB
    group = lanes_of((SUB, LANES)) // step
    out = None
    for r in range(SUB):
        part = tile[SUB * r : SUB * (r + 1), :]
        shift = (step * r - start) % LANES
        if not isinstance(shift, int) or shift:
            part = pltpu.roll(part, shift, 1)
        out = part if out is None else jnp.where(group == r, part, out)
    return out


def unpack_tail(tail, start):
    step = LANES // SUB
    parts = []
    for r in range(SUB):
        shift = (start - step * r) % LANES
        moved = not isinstance(shift, int) or shift
        parts.append(pltpu.roll(tail, shift, 1) if moved else tail)
    return jnp.concatenate(parts, axis=0)


def backward_kernel(steps, *refs, packed):
    if packed:
        (where_ref, hidden_h, w_h, gain_h, down_h, up_h, cot_h, first_h, second_h) = refs[:9]
        (keep_ref, send_ref, own_ref) = refs[9:12]
        (hidden, w, gain, down, up, cot, project_s, grad_s, back_s, turned, grads_s, first_s, second_s, sems) = refs[12:]
    else:
        (where_ref, hidden_h, w_h, gain_h, down_h, up_h, cot_h) = refs[:7]
        grads_s = refs[7]
        (hidden, w, gain, down, up, cot, project_s, grad_s, back_s, turned, sems) = refs[8:]
    tokens, model_width = hidden_h.shape
    width = w.shape[2]
    head = gain.shape[1]
    rank, features = up.shape
    full = model_width + rank
    piece = model_width // PIECES

    def block(ref, j):
        return ref.at[:, pl.ds(pl.multiple_of(j * width, width), width)]

    def part(ref, i):
        return ref.at[:, pl.ds(pl.multiple_of(i * piece, piece), piece)]

    def hidden_copy(i):
        return pltpu.make_async_copy(part(hidden_h, i), part(hidden, i), sems.at[i])

    def w_copy(j):
        return pltpu.make_async_copy(block(w_h, j), w.at[j, :model_width], sems.at[PIECES + j])

    def up_copy(j):
        return pltpu.make_async_copy(
            block(up_h, j), w.at[j, model_width:full], sems.at[PIECES + steps + j]
        )

    def cot_copy(j):
        return pltpu.make_async_copy(block(cot_h, j), cot.at[j], sems.at[PIECES + 2 * steps + j])

    single = [(down_h, down), (gain_h, gain), (up_h, up)]
    if packed:
        single += [(first_h, first_s), (second_h, second_s)]
    single = [
        pltpu.make_async_copy(source, target, sems.at[PIECES + 3 * steps + n])
        for n, (source, target) in enumerate(single)
    ]

    def each(n, body):
        lax.fori_loop(0, n, lambda i, _: body(i), None)

    single[0].start()
    each(PIECES, lambda i: hidden_copy(i).start())
    single[1].start()

    def start_block(j):
        up_copy(j).start()
        cot_copy(j).start()
        w_copy(j).start()

    each(steps, start_block)
    for copy in single[2:]:
        copy.start()

    back_s[...] = jnp.zeros_like(back_s)
    single[0].wait()

    def add_low(i):
        hidden_copy(i).wait()
        back_s[...] += lax.dot_general(
            part(hidden, i)[...],
            part(down, i)[...],
            (((1,), (1,)), ((), ())),
            preferred_element_type=F32,
        )

    each(PIECES, add_low)
    low = back_s[...].astype(BF16)
    scaled = (low.astype(F32) * adapter_scale_factor).astype(BF16)
    hidden[:, model_width:] = scaled
    turned[...] = scaled.T
    single[1].wait()

    def normalise(j):
        for h in range(width // head):
            place = slice(h * head, (h + 1) * head)
            mine = project_s[:, place]
            upstream = cot[j, :, place].astype(F32) * gain[...]
            inverse = lax.rsqrt(jnp.mean(mine * mine, axis=-1, keepdims=True) + norm_epsilon)
            normed = mine * inverse
            mean = jnp.mean(upstream * normed, axis=-1, keepdims=True)
            place = pl.ds(pl.multiple_of(j * width + h * head, head), head)
            grad_s[:, place] = (inverse * (upstream - normed * mean)).astype(BF16)

    def step(j, _):
        w_copy(j).wait()
        up_copy(j).wait()
        cot_copy(j).wait()
        before = jnp.maximum(j - 1, 0)
        normalise(before)
        project_s[...] = jnp.dot(hidden[...], w[j], preferred_element_type=F32)

    project_s[...] = jnp.zeros_like(project_s)
    lax.fori_loop(0, steps, step, None)
    single[2].wait()
    normalise(steps - 1)
    done = model_width + features - width
    grads_s[:, model_width:done] = jnp.dot(
        turned[...], grad_s[:, : features - width], preferred_element_type=F32
    )
    back = lax.dot_general(
        grad_s[...], up[...], (((1,), (1,)), ((), ())), preferred_element_type=F32
    )
    back_low = (adapter_scale_factor * back).astype(BF16).T
    grads_s[:, done:] = jnp.dot(
        turned[...], grad_s[:, features - width :], preferred_element_type=F32
    )
    turned[...] = back_low
    half = model_width // 2

    def down_half(i):
        place = pl.ds(pl.multiple_of(i * half, half), half)
        grads_s[:, place] = jnp.dot(turned[...], hidden[:, place], preferred_element_type=F32)

    each(2, down_half)
    if packed:
        for copy in single[3:]:
            copy.wait()
        pack_blocks(where_ref, grads_s, down, up, first_s, second_s, keep_ref, send_ref, own_ref)


def pack_blocks(where_ref, grads_s, down, up, first_s, second_s, keep_ref, send_ref, own_ref):
    lane = lanes_of((64, LANES))
    core = where_ref[1]
    on_zero = jnp.full((SUB, LANES), core, jnp.int32) == 0
    on_zero_main = jnp.full((64, LANES), core, jnp.int32) == 0

    def tile_of(t):
        return grads_s[:, t * LANES : (t + 1) * LANES]

    def block_of(group, j):
        a, b = tile_of(group * (SUB + 1) + j), tile_of(group * (SUB + 1) + j + 1)
        main = jnp.where(lane >= 16 * j, a, b) if j else a
        return main, pack_tail(b, 16 * j)

    def pack_group(group):
        for k in range(SUB // 2):
            even, odd = block_of(group, 2 * k), block_of(group, 2 * k + 1)
            chip = group * (SUB // 2) + k
            for ref, (one, two) in ((keep_ref, (even, odd)), (send_ref, (odd, even))):
                ref[chip, :64] = jnp.where(on_zero_main, one[0], two[0])
                ref[chip, 64:72] = jnp.where(on_zero, one[1], two[1])

    for group in reversed(range(keep_ref.shape[0] // (SUB // 2))):
        pack_group(group)

    index = where_ref[0]
    j = index % SUB
    tile = index // SUB * (SUB + 1) + j
    tiles = down.shape[1] // LANES

    def params_at(t):
        t_down = jnp.minimum(t, tiles - 1)
        t_up = jnp.maximum(t - tiles, 0)
        a = down[:, pl.ds(pl.multiple_of(t_down * LANES, LANES), LANES)].astype(F32)
        b = up[:, pl.ds(pl.multiple_of(t_up * LANES, LANES), LANES)].astype(F32)
        return jnp.where(jnp.full((64, LANES), t, jnp.int32) < tiles, a, b)

    a, b = params_at(tile), params_at(tile + 1)
    own_ref[0, :64] = jnp.where(lane >= 16 * j, a, b)
    own_ref[0, 64:72] = pack_tail(b, 16 * j)
    for n, ref in ((1, first_s), (2, second_s)):
        own_ref[n, :64] = pltpu.roll(ref[:, :LANES], 16 * j, 1)
        last = jnp.concatenate([ref[:, LANES:], jnp.zeros((64, LANES - 16), F32)], axis=1)
        own_ref[n, 64:72] = pack_tail(last, 0)


def finish_kernel(where_ref, mine_ref, other_ref, own_ref, down_ref, up_ref, first_ref, second_ref):
    lane = lanes_of((64, LANES))
    core = where_ref[1]
    on_zero = jnp.full((72, LANES), core, jnp.int32) == 0
    down_tiles = down_ref.shape[1] // LANES
    blocks = {}

    def block_of(i):
        if i not in blocks:
            blocks.clear()
            k = i // 2
            one, two = mine_ref[k].astype(F32), other_ref[k].astype(F32)
            blocks[2 * k] = jnp.where(on_zero, one, two)
            blocks[2 * k + 1] = jnp.where(on_zero, two, one)
        return blocks[i]

    tiles = (down_ref.shape[1] + up_ref.shape[1]) // LANES
    before = None
    for tile in range(tiles):
        group, t = tile // (SUB + 1), tile % (SUB + 1)
        value = None
        if t < SUB:
            value = block_of(SUB * group + t)
        out = value[:64] if t == 0 else None
        if t:
            out = unpack_tail(before[64:72], 16 * (t - 1))
            if t > 1:
                out = jnp.where(lane < 16 * (t - 1), before[:64], out)
            if t < SUB:
                out = jnp.where(lane >= 16 * t, value[:64], out)
        before = value
        out = out.astype(BF16)
        if tile < down_tiles:
            down_ref[:, tile * LANES : (tile + 1) * LANES] = out
        else:
            up_ref[:, (tile - down_tiles) * LANES : (tile - down_tiles + 1) * LANES] = out

    j = where_ref[0] % SUB
    for n, ref in ((0, first_ref), (1, second_ref)):
        ref[:, :LANES] = pltpu.roll(own_ref[n, :64], (LANES - 16 * j) % LANES, 1)
        ref[:, LANES:] = unpack_tail(own_ref[n, 64:72], 0)[:, :16]


def backward(where, hidden, w_query, gain, down_t, up, cotangent, first_t, second_t, chips, packed):
    tokens, model_width = hidden.shape
    features = w_query.shape[1]
    rank = down_t.shape[0]
    head = gain.shape[1]
    width = 2 * head if features % (2 * head) == 0 else head
    steps = features // width
    rows = model_width + features
    depth = model_width + rank
    far = pl.BlockSpec(memory_space=pltpu.HBM)
    near = pl.BlockSpec(memory_space=pltpu.VMEM)
    operands = [hidden, w_query, gain, down_t, up, cotangent]
    scratch = [
        pltpu.VMEM((tokens, depth), BF16),
        pltpu.VMEM((steps, depth, width), BF16),
        pltpu.VMEM((1, head), F32),
        pltpu.VMEM((rank, model_width), BF16),
        pltpu.VMEM((rank, features), BF16),
        pltpu.VMEM((steps, tokens, width), BF16),
        pltpu.VMEM((tokens, width), F32),
        pltpu.VMEM((tokens, features), BF16),
        pltpu.VMEM((tokens, rank), F32),
        pltpu.VMEM((rank, tokens), BF16),
    ]
    if packed:
        own = rows // chips // 2
        height = rank * own // LANES
        halves = (chips, height, LANES)
        operands += [first_t, second_t]
        out_shape = [jax.ShapeDtypeStruct(halves, F32)] * 2 + [
            jax.ShapeDtypeStruct((3, height, LANES), F32)
        ]
        out_specs = [near] * 3
        scratch += [pltpu.VMEM((rank, rows), F32)] + [pltpu.VMEM((rank, own), F32)] * 2
    else:
        out_shape = jax.ShapeDtypeStruct((rank, rows), F32)
        out_specs = near
    scratch += [pltpu.SemaphoreType.DMA((3 * steps + PIECES + 5,))]
    operands = [pltpu.with_memory_space_constraint(x, pltpu.HBM) for x in operands]
    return pl.pallas_call(
        functools.partial(backward_kernel, steps, packed=packed),
        in_specs=[pl.BlockSpec(memory_space=pltpu.SMEM)] + [far] * len(operands),
        out_specs=out_specs,
        out_shape=out_shape,
        scratch_shapes=scratch,
        compiler_params=pltpu.CompilerParams(vmem_limit_bytes=32 << 20),
        name="backward",
    )(where, *operands)


def finish(where, mine, other, own_new, model_width, features):
    rank = 64
    own = own_new.shape[1] * LANES // rank
    full = pl.BlockSpec(memory_space=pltpu.VMEM)
    return pl.pallas_call(
        finish_kernel,
        in_specs=[pl.BlockSpec(memory_space=pltpu.SMEM), full, full, full],
        out_specs=[full] * 4,
        out_shape=[
            jax.ShapeDtypeStruct((rank, model_width), BF16),
            jax.ShapeDtypeStruct((rank, features), BF16),
            jax.ShapeDtypeStruct((rank, own), F32),
            jax.ShapeDtypeStruct((rank, own), F32),
        ],
        compiler_params=pltpu.CompilerParams(vmem_limit_bytes=32 << 20),
        name="finish",
    )(where, mine, other, own_new)


def coded_of(g):
    g = g * RANGE
    return (g * lax.rsqrt(jnp.maximum(jnp.abs(g), TINY))).astype(jnp.float16)


def decoded_of(code):
    root = code.astype(F32)
    return root * jnp.abs(root)


def rows_of(columns):
    return columns.reshape(-1, LANES)


def on_device(
    hidden_in,
    w_query,
    query_gain,
    down_projection_matrix,
    up_projection_matrix,
    query_cotangent,
    first_moment,
    second_moment,
):
    model_width, rank = down_projection_matrix.shape
    features = up_projection_matrix.shape[1]
    chips = lax.axis_size(CHIPS)
    devices = 2 * chips
    own = (model_width + features) // devices
    height = rank * own // LANES
    packed = rank == 64 and own == LANES + 16 and model_width % LANES == 0 and chips % 4 == 0
    core = lax.axis_index("core")
    index = lax.axis_index(EVERY)
    where = jnp.stack([index, core]).astype(jnp.int32)
    down_t = down_projection_matrix.T
    result = backward(
        where,
        hidden_in,
        w_query,
        query_gain[None, :],
        down_t,
        up_projection_matrix,
        query_cotangent,
        first_moment.T,
        second_moment.T,
        chips,
        packed,
    )
    if packed:
        keep, send, own_state = result
        params, first, second = own_state[0], own_state[1], own_state[2]
    else:
        blocks = result.reshape(rank, chips, 2, own).transpose(2, 1, 0, 3).reshape(2, chips, -1, LANES)
        keep = lax.dynamic_index_in_dim(blocks, core, 0, keepdims=False)
        send = lax.dynamic_index_in_dim(blocks, 1 - core, 0, keepdims=False)
        combined = jnp.concatenate([down_t, up_projection_matrix], axis=1)
        params = rows_of(lax.dynamic_slice_in_dim(combined, index * own, own, 1)).astype(F32)
        first, second = rows_of(first_moment.T), rows_of(second_moment.T)

    other = decoded_of(lax.ppermute(coded_of(send), "core", SWAP)) / RANGE
    coded = coded_of(keep + other)
    arrived = lax.all_to_all(coded, CHIPS, 0, 0, tiled=True)
    grads = None
    for k in range(chips):
        term = decoded_of(arrived[k])
        grads = term if grads is None else grads + term
    grads = grads / (RANGE * devices)
    first_new = beta_one * first + (1.0 - beta_one) * grads
    second_new = beta_two * second + (1.0 - beta_two) * grads * grads
    direction = first_new / first_bias / (jnp.sqrt(second_new / second_bias) + adam_eps)
    updated = (params - learn_rate * direction).astype(BF16)

    copies = jnp.broadcast_to(updated[None], (chips, height, LANES))
    copies, first_new, second_new = lax.optimization_barrier((copies, first_new, second_new))
    mine = lax.all_to_all(copies, CHIPS, 0, 0, tiled=True)
    other = lax.ppermute(mine, "core", SWAP)
    if packed:
        own_new = jnp.stack([first_new, second_new])
        down_new, up_new, first_out, second_out = finish(where, mine, other, own_new, model_width, features)
    else:
        pair = jnp.stack([mine, other])
        pair = jnp.where(core == 0, pair, pair[::-1])
        columns = pair.reshape(2, chips, rank, own).transpose(2, 1, 0, 3).reshape(rank, devices * own)
        down_new, up_new = columns[:, :model_width], columns[:, model_width:]
        first_out, second_out = first_new.reshape(rank, own), second_new.reshape(rank, own)
    return (down_new.T, up_new, first_out.T, second_out.T)


def solution(mesh):
    groups, replicas = mesh.shape["group"], mesh.shape["replica"]
    fine = Mesh(mesh.devices.reshape(groups, replicas // 2, 2), EVERY)
    rows = P(EVERY, None)
    return jax.shard_map(
        on_device,
        mesh=fine,
        in_specs=(rows, P(), P(), P(), P(), rows, rows, rows),
        out_specs=(P(), P(), rows, rows),
        check_vma=False,
    )
```

```python
import functools

import jax
import jax.numpy as jnp
from jax import lax
from jax.experimental import pallas as pl
from jax.experimental.pallas import tpu as pltpu
from jax.sharding import Mesh
from jax.sharding import PartitionSpec as P

adapter_scale_factor = 0.5
norm_epsilon = 1e-06
beta_one = 0.9
beta_two = 0.999
first_bias = 1.0 - 0.9**10
second_bias = 1.0 - 0.999**10
learn_rate = 0.001
adam_eps = 1e-08

LANES = 128
SUB = 8
RANGE = 2.0**-11
TINY = 2.0**-100
PIECES = 2
F32 = jnp.float32
BF16 = jnp.bfloat16
EVERY = ("group", "chip", "core")
CHIPS = ("group", "chip")
SWAP = ((0, 1), (1, 0))


def lanes_of(shape):
    return lax.broadcasted_iota(jnp.int32, shape, len(shape) - 1)


def pack_tail(tile, start):
    step = LANES // SUB
    group = lanes_of((SUB, LANES)) // step
    out = None
    for r in range(SUB):
        part = tile[SUB * r : SUB * (r + 1), :]
        shift = (step * r - start) % LANES
        if not isinstance(shift, int) or shift:
            part = pltpu.roll(part, shift, 1)
        out = part if out is None else jnp.where(group == r, part, out)
    return out


def unpack_tail(tail, start):
    step = LANES // SUB
    parts = []
    for r in range(SUB):
        shift = (start - step * r) % LANES
        moved = not isinstance(shift, int) or shift
        parts.append(pltpu.roll(tail, shift, 1) if moved else tail)
    return jnp.concatenate(parts, axis=0)


def backward_kernel(steps, *refs, packed):
    if packed:
        (hidden_h, w_h, gain_h, down_h, up_h, cot_h, first_h, second_h) = refs[:8]
        (keep_ref, send_ref, own_ref) = refs[8:11]
        (hidden, w, gain, down, up, cot, project_s, grad_s, back_s, turned, grads_s, first_s, second_s, sems) = refs[11:]
    else:
        (hidden_h, w_h, gain_h, down_h, up_h, cot_h) = refs[:6]
        grads_s = refs[6]
        (hidden, w, gain, down, up, cot, project_s, grad_s, back_s, turned, sems) = refs[7:]
    tokens, model_width = hidden_h.shape
    width = w.shape[2]
    head = gain.shape[1]
    rank, features = up.shape
    full = model_width + rank
    piece = model_width // PIECES

    def block(ref, j):
        return ref.at[:, pl.ds(pl.multiple_of(j * width, width), width)]

    def part(ref, i):
        return ref.at[:, pl.ds(pl.multiple_of(i * piece, piece), piece)]

    def hidden_copy(i):
        return pltpu.make_async_copy(part(hidden_h, i), part(hidden, i), sems.at[i])

    def w_copy(j):
        return pltpu.make_async_copy(block(w_h, j), w.at[j, :model_width], sems.at[PIECES + j])

    def up_copy(j):
        return pltpu.make_async_copy(
            block(up_h, j), w.at[j, model_width:full], sems.at[PIECES + steps + j]
        )

    def cot_copy(j):
        return pltpu.make_async_copy(block(cot_h, j), cot.at[j], sems.at[PIECES + 2 * steps + j])

    single = [(down_h, down), (gain_h, gain), (up_h, up)]
    if packed:
        single += [(first_h, first_s), (second_h, second_s)]
    single = [
        pltpu.make_async_copy(source, target, sems.at[PIECES + 3 * steps + n])
        for n, (source, target) in enumerate(single)
    ]

    def each(n, body):
        lax.fori_loop(0, n, lambda i, _: body(i), None)

    single[0].start()
    each(PIECES, lambda i: hidden_copy(i).start())
    single[1].start()

    def start_block(j):
        up_copy(j).start()
        cot_copy(j).start()
        w_copy(j).start()

    each(steps, start_block)
    for copy in single[2:]:
        copy.start()

    back_s[...] = jnp.zeros_like(back_s)
    single[0].wait()

    def add_low(i):
        hidden_copy(i).wait()
        back_s[...] += lax.dot_general(
            part(hidden, i)[...],
            part(down, i)[...],
            (((1,), (1,)), ((), ())),
            preferred_element_type=F32,
        )

    each(PIECES, add_low)
    low = back_s[...].astype(BF16)
    scaled = (low.astype(F32) * adapter_scale_factor).astype(BF16)
    hidden[:, model_width:] = scaled
    turned[...] = scaled.T
    single[1].wait()

    def normalise(j):
        for h in range(width // head):
            place = slice(h * head, (h + 1) * head)
            mine = project_s[:, place]
            upstream = cot[j, :, place].astype(F32) * gain[...]
            inverse = lax.rsqrt(jnp.mean(mine * mine, axis=-1, keepdims=True) + norm_epsilon)
            normed = mine * inverse
            mean = jnp.mean(upstream * normed, axis=-1, keepdims=True)
            place = pl.ds(pl.multiple_of(j * width + h * head, head), head)
            grad_s[:, place] = (inverse * (upstream - normed * mean)).astype(BF16)

    def step(j, _):
        w_copy(j).wait()
        up_copy(j).wait()
        cot_copy(j).wait()
        before = jnp.maximum(j - 1, 0)
        normalise(before)
        project_s[...] = jnp.dot(hidden[...], w[j], preferred_element_type=F32)

    project_s[...] = jnp.zeros_like(project_s)
    lax.fori_loop(0, steps, step, None)
    single[2].wait()
    normalise(steps - 1)
    done = model_width + features - width
    grads_s[:, model_width:done] = jnp.dot(
        turned[...], grad_s[:, : features - width], preferred_element_type=F32
    )
    back = lax.dot_general(
        grad_s[...], up[...], (((1,), (1,)), ((), ())), preferred_element_type=F32
    )
    back_low = (adapter_scale_factor * back).astype(BF16).T
    grads_s[:, done:] = jnp.dot(
        turned[...], grad_s[:, features - width :], preferred_element_type=F32
    )
    turned[...] = back_low
    half = model_width // 2

    def down_half(i):
        place = pl.ds(pl.multiple_of(i * half, half), half)
        grads_s[:, place] = jnp.dot(turned[...], hidden[:, place], preferred_element_type=F32)

    each(2, down_half)
    if packed:
        for copy in single[3:]:
            copy.wait()
        pack_blocks(grads_s, down, up, first_s, second_s, keep_ref, send_ref, own_ref)


def pack_blocks(grads_s, down, up, first_s, second_s, keep_ref, send_ref, own_ref):
    lane = lanes_of((64, LANES))
    core = lax.axis_index("core")
    on_zero = jnp.full((SUB, LANES), core, jnp.int32) == 0
    on_zero_main = jnp.full((64, LANES), core, jnp.int32) == 0

    def tile_of(t):
        return grads_s[:, t * LANES : (t + 1) * LANES]

    def block_of(group, j):
        a, b = tile_of(group * (SUB + 1) + j), tile_of(group * (SUB + 1) + j + 1)
        main = jnp.where(lane >= 16 * j, a, b) if j else a
        return main, pack_tail(b, 16 * j)

    def pack_group(group):
        for k in range(SUB // 2):
            even, odd = block_of(group, 2 * k), block_of(group, 2 * k + 1)
            chip = group * (SUB // 2) + k
            for ref, (one, two) in ((keep_ref, (even, odd)), (send_ref, (odd, even))):
                ref[chip, :64] = jnp.where(on_zero_main, one[0], two[0])
                ref[chip, 64:72] = jnp.where(on_zero, one[1], two[1])

    for group in reversed(range(keep_ref.shape[0] // (SUB // 2))):
        pack_group(group)

    index = lax.axis_index(EVERY)
    j = index % SUB
    tile = index // SUB * (SUB + 1) + j
    tiles = down.shape[1] // LANES

    def params_at(t):
        t_down = jnp.minimum(t, tiles - 1)
        t_up = jnp.maximum(t - tiles, 0)
        a = down[:, pl.ds(pl.multiple_of(t_down * LANES, LANES), LANES)].astype(F32)
        b = up[:, pl.ds(pl.multiple_of(t_up * LANES, LANES), LANES)].astype(F32)
        return jnp.where(jnp.full((64, LANES), t, jnp.int32) < tiles, a, b)

    a, b = params_at(tile), params_at(tile + 1)
    own_ref[0, :64] = jnp.where(lane >= 16 * j, a, b)
    own_ref[0, 64:72] = pack_tail(b, 16 * j)
    for n, ref in ((1, first_s), (2, second_s)):
        own_ref[n, :64] = pltpu.roll(ref[:, :LANES], 16 * j, 1)
        last = jnp.concatenate([ref[:, LANES:], jnp.zeros((64, LANES - 16), F32)], axis=1)
        own_ref[n, 64:72] = pack_tail(last, 0)


def finish_kernel(mine_ref, other_ref, own_ref, down_ref, up_ref, first_ref, second_ref):
    lane = lanes_of((64, LANES))
    core = lax.axis_index("core")
    on_zero = jnp.full((72, LANES), core, jnp.int32) == 0
    down_tiles = down_ref.shape[1] // LANES
    blocks = {}

    def block_of(i):
        if i not in blocks:
            blocks.clear()
            k = i // 2
            one, two = mine_ref[k].astype(F32), other_ref[k].astype(F32)
            blocks[2 * k] = jnp.where(on_zero, one, two)
            blocks[2 * k + 1] = jnp.where(on_zero, two, one)
        return blocks[i]

    tiles = (down_ref.shape[1] + up_ref.shape[1]) // LANES
    before = None
    for tile in range(tiles):
        group, t = tile // (SUB + 1), tile % (SUB + 1)
        value = None
        if t < SUB:
            value = block_of(SUB * group + t)
        out = value[:64] if t == 0 else None
        if t:
            out = unpack_tail(before[64:72], 16 * (t - 1))
            if t > 1:
                out = jnp.where(lane < 16 * (t - 1), before[:64], out)
            if t < SUB:
                out = jnp.where(lane >= 16 * t, value[:64], out)
        before = value
        out = out.astype(BF16)
        if tile < down_tiles:
            down_ref[:, tile * LANES : (tile + 1) * LANES] = out
        else:
            up_ref[:, (tile - down_tiles) * LANES : (tile - down_tiles + 1) * LANES] = out

    j = lax.axis_index(EVERY) % SUB
    for n, ref in ((0, first_ref), (1, second_ref)):
        ref[:, :LANES] = pltpu.roll(own_ref[n, :64], (LANES - 16 * j) % LANES, 1)
        ref[:, LANES:] = unpack_tail(own_ref[n, 64:72], 0)[:, :16]


def backward(hidden, w_query, gain, down_t, up, cotangent, first_t, second_t, chips, packed):
    tokens, model_width = hidden.shape
    features = w_query.shape[1]
    rank = down_t.shape[0]
    head = gain.shape[1]
    width = 2 * head if features % (2 * head) == 0 else head
    steps = features // width
    rows = model_width + features
    depth = model_width + rank
    far = pl.BlockSpec(memory_space=pltpu.HBM)
    near = pl.BlockSpec(memory_space=pltpu.VMEM)
    operands = [hidden, w_query, gain, down_t, up, cotangent]
    scratch = [
        pltpu.VMEM((tokens, depth), BF16),
        pltpu.VMEM((steps, depth, width), BF16),
        pltpu.VMEM((1, head), F32),
        pltpu.VMEM((rank, model_width), BF16),
        pltpu.VMEM((rank, features), BF16),
        pltpu.VMEM((steps, tokens, width), BF16),
        pltpu.VMEM((tokens, width), F32),
        pltpu.VMEM((tokens, features), BF16),
        pltpu.VMEM((tokens, rank), F32),
        pltpu.VMEM((rank, tokens), BF16),
    ]
    if packed:
        own = rows // chips // 2
        height = rank * own // LANES
        halves = (chips, height, LANES)
        operands += [first_t, second_t]
        out_shape = [jax.ShapeDtypeStruct(halves, F32)] * 2 + [
            jax.ShapeDtypeStruct((3, height, LANES), F32)
        ]
        out_specs = [near] * 3
        scratch += [pltpu.VMEM((rank, rows), F32)] + [pltpu.VMEM((rank, own), F32)] * 2
    else:
        out_shape = jax.ShapeDtypeStruct((rank, rows), F32)
        out_specs = near
    scratch += [pltpu.SemaphoreType.DMA((3 * steps + PIECES + 5,))]
    operands = [pltpu.with_memory_space_constraint(x, pltpu.HBM) for x in operands]
    return pl.pallas_call(
        functools.partial(backward_kernel, steps, packed=packed),
        in_specs=[far] * len(operands),
        out_specs=out_specs,
        out_shape=out_shape,
        scratch_shapes=scratch,
        compiler_params=pltpu.CompilerParams(vmem_limit_bytes=32 << 20),
        name="backward",
    )(*operands)


def finish(mine, other, own_new, model_width, features):
    rank = 64
    own = own_new.shape[1] * LANES // rank
    full = pl.BlockSpec(memory_space=pltpu.VMEM)
    return pl.pallas_call(
        finish_kernel,
        in_specs=[full, full, full],
        out_specs=[full] * 4,
        out_shape=[
            jax.ShapeDtypeStruct((rank, model_width), BF16),
            jax.ShapeDtypeStruct((rank, features), BF16),
            jax.ShapeDtypeStruct((rank, own), F32),
            jax.ShapeDtypeStruct((rank, own), F32),
        ],
        compiler_params=pltpu.CompilerParams(vmem_limit_bytes=32 << 20),
        name="finish",
    )(mine, other, own_new)


def coded_of(g):
    g = g * RANGE
    return (g * lax.rsqrt(jnp.maximum(jnp.abs(g), TINY))).astype(jnp.float16)


def decoded_of(code):
    root = code.astype(F32)
    return root * jnp.abs(root)


def rows_of(columns):
    return columns.reshape(-1, LANES)


def on_device(
    hidden_in,
    w_query,
    query_gain,
    down_projection_matrix,
    up_projection_matrix,
    query_cotangent,
    first_moment,
    second_moment,
):
    model_width, rank = down_projection_matrix.shape
    features = up_projection_matrix.shape[1]
    chips = lax.axis_size(CHIPS)
    devices = 2 * chips
    own = (model_width + features) // devices
    height = rank * own // LANES
    packed = rank == 64 and own == LANES + 16 and model_width % LANES == 0 and chips % 4 == 0
    core = lax.axis_index("core")
    index = lax.axis_index(EVERY)
    down_t = down_projection_matrix.T
    result = backward(
        hidden_in,
        w_query,
        query_gain[None, :],
        down_t,
        up_projection_matrix,
        query_cotangent,
        first_moment.T,
        second_moment.T,
        chips,
        packed,
    )
    if packed:
        keep, send, own_state = result
        params, first, second = own_state[0], own_state[1], own_state[2]
    else:
        blocks = result.reshape(rank, chips, 2, own).transpose(2, 1, 0, 3).reshape(2, chips, -1, LANES)
        keep = lax.dynamic_index_in_dim(blocks, core, 0, keepdims=False)
        send = lax.dynamic_index_in_dim(blocks, 1 - core, 0, keepdims=False)
        combined = jnp.concatenate([down_t, up_projection_matrix], axis=1)
        params = rows_of(lax.dynamic_slice_in_dim(combined, index * own, own, 1)).astype(F32)
        first, second = rows_of(first_moment.T), rows_of(second_moment.T)

    other = decoded_of(lax.ppermute(coded_of(send), "core", SWAP)) / RANGE
    coded = coded_of(keep + other)
    arrived = lax.all_to_all(coded, CHIPS, 0, 0, tiled=True)
    grads = None
    for k in range(chips):
        term = decoded_of(arrived[k])
        grads = term if grads is None else grads + term
    grads = grads / (RANGE * devices)
    first_new = beta_one * first + (1.0 - beta_one) * grads
    second_new = beta_two * second + (1.0 - beta_two) * grads * grads
    direction = first_new / first_bias / (jnp.sqrt(second_new / second_bias) + adam_eps)
    updated = (params - learn_rate * direction).astype(BF16)

    copies = jnp.broadcast_to(updated[None], (chips, height, LANES))
    copies, first_new, second_new = lax.optimization_barrier((copies, first_new, second_new))
    mine = lax.all_to_all(copies, CHIPS, 0, 0, tiled=True)
    other = lax.ppermute(mine, "core", SWAP)
    if packed:
        own_new = jnp.stack([first_new, second_new])
        down_new, up_new, first_out, second_out = finish(mine, other, own_new, model_width, features)
    else:
        pair = jnp.stack([mine, other])
        pair = jnp.where(core == 0, pair, pair[::-1])
        columns = pair.reshape(2, chips, rank, own).transpose(2, 1, 0, 3).reshape(rank, devices * own)
        down_new, up_new = columns[:, :model_width], columns[:, model_width:]
        first_out, second_out = first_new.reshape(rank, own), second_new.reshape(rank, own)
    return (down_new.T, up_new, first_out.T, second_out.T)


def solution(mesh):
    groups, replicas = mesh.shape["group"], mesh.shape["replica"]
    fine = Mesh(mesh.devices.reshape(groups, replicas // 2, 2), EVERY)
    rows = P(EVERY, None)
    return jax.shard_map(
        on_device,
        mesh=fine,
        in_specs=(rows, P(), P(), P(), P(), rows, rows, rows),
        out_specs=(P(), P(), rows, rows),
        check_vma=False,
    )
```

```python
import functools

import jax
import jax.numpy as jnp
from jax import lax
from jax.experimental import pallas as pl
from jax.experimental.pallas import tpu as pltpu
from jax.sharding import Mesh
from jax.sharding import PartitionSpec as P

adapter_scale_factor = 0.5
norm_epsilon = 1e-06
beta_one = 0.9
beta_two = 0.999
first_bias = 1.0 - 0.9**10
second_bias = 1.0 - 0.999**10
learn_rate = 0.001
adam_eps = 1e-08

LANES = 128
SUB = 8
RANGE = 2.0**-11
TINY = 2.0**-100
PIECES = 2
F32 = jnp.float32
BF16 = jnp.bfloat16
EVERY = ("group", "chip", "core")
CHIPS = ("group", "chip")
SWAP = ((0, 1), (1, 0))


def lanes_of(shape):
    return lax.broadcasted_iota(jnp.int32, shape, len(shape) - 1)


def pack_tail(tile, start):
    step = LANES // SUB
    group = lanes_of((SUB, LANES)) // step
    out = None
    for r in range(SUB):
        part = tile[SUB * r : SUB * (r + 1), :]
        shift = (step * r - start) % LANES
        if not isinstance(shift, int) or shift:
            part = pltpu.roll(part, shift, 1)
        out = part if out is None else jnp.where(group == r, part, out)
    return out


def unpack_tail(tail, start):
    step = LANES // SUB
    parts = []
    for r in range(SUB):
        shift = (start - step * r) % LANES
        moved = not isinstance(shift, int) or shift
        parts.append(pltpu.roll(tail, shift, 1) if moved else tail)
    return jnp.concatenate(parts, axis=0)


def backward_kernel(steps, *refs, packed):
    if packed:
        (hidden_h, w_h, gain_h, down_h, up_h, cot_h, first_h, second_h) = refs[:8]
        (both_ref, own_ref) = refs[8:10]
        (hidden, w, gain, down, up, cot, project_s, grad_s, back_s, turned, grads_s, first_s, second_s, sems) = refs[10:]
    else:
        (hidden_h, w_h, gain_h, down_h, up_h, cot_h) = refs[:6]
        grads_s = refs[6]
        (hidden, w, gain, down, up, cot, project_s, grad_s, back_s, turned, sems) = refs[7:]
    tokens, model_width = hidden_h.shape
    width = w.shape[2]
    head = gain.shape[1]
    rank, features = up.shape
    full = model_width + rank
    piece = model_width // PIECES

    def block(ref, j):
        return ref.at[:, pl.ds(pl.multiple_of(j * width, width), width)]

    def part(ref, i):
        return ref.at[:, pl.ds(pl.multiple_of(i * piece, piece), piece)]

    def hidden_copy(i):
        return pltpu.make_async_copy(part(hidden_h, i), part(hidden, i), sems.at[i])

    def w_copy(j):
        return pltpu.make_async_copy(block(w_h, j), w.at[j, :model_width], sems.at[PIECES + j])

    def up_copy(j):
        return pltpu.make_async_copy(
            block(up_h, j), w.at[j, model_width:full], sems.at[PIECES + steps + j]
        )

    def cot_copy(j):
        return pltpu.make_async_copy(block(cot_h, j), cot.at[j], sems.at[PIECES + 2 * steps + j])

    single = [(down_h, down), (gain_h, gain), (up_h, up)]
    if packed:
        single += [(first_h, first_s), (second_h, second_s)]
    single = [
        pltpu.make_async_copy(source, target, sems.at[PIECES + 3 * steps + n])
        for n, (source, target) in enumerate(single)
    ]

    def each(n, body):
        lax.fori_loop(0, n, lambda i, _: body(i), None)

    single[0].start()
    each(PIECES, lambda i: hidden_copy(i).start())
    single[1].start()

    def start_block(j):
        up_copy(j).start()
        cot_copy(j).start()
        w_copy(j).start()

    each(steps, start_block)
    for copy in single[2:]:
        copy.start()

    back_s[...] = jnp.zeros_like(back_s)
    single[0].wait()

    def add_low(i):
        hidden_copy(i).wait()
        back_s[...] += lax.dot_general(
            part(hidden, i)[...],
            part(down, i)[...],
            (((1,), (1,)), ((), ())),
            preferred_element_type=F32,
        )

    each(PIECES, add_low)
    low = back_s[...].astype(BF16)
    scaled = (low.astype(F32) * adapter_scale_factor).astype(BF16)
    hidden[:, model_width:] = scaled
    turned[...] = scaled.T
    single[1].wait()

    def normalise(j):
        for h in range(width // head):
            place = slice(h * head, (h + 1) * head)
            mine = project_s[:, place]
            upstream = cot[j, :, place].astype(F32) * gain[...]
            inverse = lax.rsqrt(jnp.mean(mine * mine, axis=-1, keepdims=True) + norm_epsilon)
            normed = mine * inverse
            mean = jnp.mean(upstream * normed, axis=-1, keepdims=True)
            place = pl.ds(pl.multiple_of(j * width + h * head, head), head)
            grad_s[:, place] = (inverse * (upstream - normed * mean)).astype(BF16)

    def step(j, _):
        w_copy(j).wait()
        up_copy(j).wait()
        cot_copy(j).wait()
        before = jnp.maximum(j - 1, 0)
        normalise(before)
        project_s[...] = jnp.dot(hidden[...], w[j], preferred_element_type=F32)

    project_s[...] = jnp.zeros_like(project_s)
    lax.fori_loop(0, steps, step, None)
    single[2].wait()
    normalise(steps - 1)
    done = model_width + features - width
    grads_s[:, model_width:done] = jnp.dot(
        turned[...], grad_s[:, : features - width], preferred_element_type=F32
    )
    back = lax.dot_general(
        grad_s[...], up[...], (((1,), (1,)), ((), ())), preferred_element_type=F32
    )
    back_low = (adapter_scale_factor * back).astype(BF16).T
    grads_s[:, done:] = jnp.dot(
        turned[...], grad_s[:, features - width :], preferred_element_type=F32
    )
    turned[...] = back_low
    half = model_width // 2

    def down_half(i):
        place = pl.ds(pl.multiple_of(i * half, half), half)
        grads_s[:, place] = jnp.dot(turned[...], hidden[:, place], preferred_element_type=F32)

    each(2, down_half)
    if packed:
        for copy in single[3:]:
            copy.wait()
        pack_blocks(grads_s, down, up, first_s, second_s, both_ref, own_ref)


def pack_blocks(grads_s, down, up, first_s, second_s, both_ref, own_ref):
    lane = lanes_of((64, LANES))

    def tile_of(t):
        return grads_s[:, t * LANES : (t + 1) * LANES]

    def block_of(group, j):
        a, b = tile_of(group * (SUB + 1) + j), tile_of(group * (SUB + 1) + j + 1)
        main = jnp.where(lane >= 16 * j, a, b) if j else a
        return main, pack_tail(b, 16 * j)

    def pack_group(group):
        for k in range(SUB // 2):
            chip = group * (SUB // 2) + k
            for core in range(2):
                main, tail = block_of(group, 2 * k + core)
                both_ref[core, chip, :64] = main
                both_ref[core, chip, 64:72] = tail

    for group in reversed(range(both_ref.shape[1] // (SUB // 2))):
        pack_group(group)

    index = lax.axis_index(EVERY)
    j = index % SUB
    tile = index // SUB * (SUB + 1) + j
    tiles = down.shape[1] // LANES

    def params_at(t):
        t_down = jnp.minimum(t, tiles - 1)
        t_up = jnp.maximum(t - tiles, 0)
        a = down[:, pl.ds(pl.multiple_of(t_down * LANES, LANES), LANES)].astype(F32)
        b = up[:, pl.ds(pl.multiple_of(t_up * LANES, LANES), LANES)].astype(F32)
        return jnp.where(jnp.full((64, LANES), t, jnp.int32) < tiles, a, b)

    a, b = params_at(tile), params_at(tile + 1)
    own_ref[0, :64] = jnp.where(lane >= 16 * j, a, b)
    own_ref[0, 64:72] = pack_tail(b, 16 * j)
    for n, ref in ((1, first_s), (2, second_s)):
        own_ref[n, :64] = pltpu.roll(ref[:, :LANES], 16 * j, 1)
        last = jnp.concatenate([ref[:, LANES:], jnp.zeros((64, LANES - 16), F32)], axis=1)
        own_ref[n, 64:72] = pack_tail(last, 0)


def finish_kernel(mine_ref, other_ref, own_ref, down_ref, up_ref, first_ref, second_ref):
    lane = lanes_of((64, LANES))
    core = lax.axis_index("core")
    on_zero = jnp.full((72, LANES), core, jnp.int32) == 0
    down_tiles = down_ref.shape[1] // LANES
    blocks = {}

    def block_of(i):
        if i not in blocks:
            blocks.clear()
            k = i // 2
            one, two = mine_ref[k].astype(F32), other_ref[k].astype(F32)
            blocks[2 * k] = jnp.where(on_zero, one, two)
            blocks[2 * k + 1] = jnp.where(on_zero, two, one)
        return blocks[i]

    tiles = (down_ref.shape[1] + up_ref.shape[1]) // LANES
    before = None
    for tile in range(tiles):
        group, t = tile // (SUB + 1), tile % (SUB + 1)
        value = None
        if t < SUB:
            value = block_of(SUB * group + t)
        out = value[:64] if t == 0 else None
        if t:
            out = unpack_tail(before[64:72], 16 * (t - 1))
            if t > 1:
                out = jnp.where(lane < 16 * (t - 1), before[:64], out)
            if t < SUB:
                out = jnp.where(lane >= 16 * t, value[:64], out)
        before = value
        out = out.astype(BF16)
        if tile < down_tiles:
            down_ref[:, tile * LANES : (tile + 1) * LANES] = out
        else:
            up_ref[:, (tile - down_tiles) * LANES : (tile - down_tiles + 1) * LANES] = out

    j = lax.axis_index(EVERY) % SUB
    for n, ref in ((0, first_ref), (1, second_ref)):
        ref[:, :LANES] = pltpu.roll(own_ref[n, :64], (LANES - 16 * j) % LANES, 1)
        ref[:, LANES:] = unpack_tail(own_ref[n, 64:72], 0)[:, :16]


def backward(hidden, w_query, gain, down_t, up, cotangent, first_t, second_t, chips, packed):
    tokens, model_width = hidden.shape
    features = w_query.shape[1]
    rank = down_t.shape[0]
    head = gain.shape[1]
    width = 2 * head if features % (2 * head) == 0 else head
    steps = features // width
    rows = model_width + features
    depth = model_width + rank
    far = pl.BlockSpec(memory_space=pltpu.HBM)
    near = pl.BlockSpec(memory_space=pltpu.VMEM)
    operands = [hidden, w_query, gain, down_t, up, cotangent]
    scratch = [
        pltpu.VMEM((tokens, depth), BF16),
        pltpu.VMEM((steps, depth, width), BF16),
        pltpu.VMEM((1, head), F32),
        pltpu.VMEM((rank, model_width), BF16),
        pltpu.VMEM((rank, features), BF16),
        pltpu.VMEM((steps, tokens, width), BF16),
        pltpu.VMEM((tokens, width), F32),
        pltpu.VMEM((tokens, features), BF16),
        pltpu.VMEM((tokens, rank), F32),
        pltpu.VMEM((rank, tokens), BF16),
    ]
    if packed:
        own = rows // chips // 2
        height = rank * own // LANES
        halves = (2, chips, height, LANES)
        operands += [first_t, second_t]
        out_shape = [
            jax.ShapeDtypeStruct(halves, F32),
            jax.ShapeDtypeStruct((3, height, LANES), F32),
        ]
        out_specs = [near] * 2
        scratch += [pltpu.VMEM((rank, rows), F32)] + [pltpu.VMEM((rank, own), F32)] * 2
    else:
        out_shape = jax.ShapeDtypeStruct((rank, rows), F32)
        out_specs = near
    scratch += [pltpu.SemaphoreType.DMA((3 * steps + PIECES + 5,))]
    operands = [pltpu.with_memory_space_constraint(x, pltpu.HBM) for x in operands]
    return pl.pallas_call(
        functools.partial(backward_kernel, steps, packed=packed),
        in_specs=[far] * len(operands),
        out_specs=out_specs,
        out_shape=out_shape,
        scratch_shapes=scratch,
        compiler_params=pltpu.CompilerParams(vmem_limit_bytes=32 << 20),
        name="backward",
    )(*operands)


def finish(mine, other, own_new, model_width, features):
    rank = 64
    own = own_new.shape[1] * LANES // rank
    full = pl.BlockSpec(memory_space=pltpu.VMEM)
    return pl.pallas_call(
        finish_kernel,
        in_specs=[full, full, full],
        out_specs=[full] * 4,
        out_shape=[
            jax.ShapeDtypeStruct((rank, model_width), BF16),
            jax.ShapeDtypeStruct((rank, features), BF16),
            jax.ShapeDtypeStruct((rank, own), F32),
            jax.ShapeDtypeStruct((rank, own), F32),
        ],
        compiler_params=pltpu.CompilerParams(vmem_limit_bytes=32 << 20),
        name="finish",
    )(mine, other, own_new)


def coded_of(g):
    g = g * RANGE
    return (g * lax.rsqrt(jnp.maximum(jnp.abs(g), TINY))).astype(jnp.float16)


def decoded_of(code):
    root = code.astype(F32)
    return root * jnp.abs(root)


def rows_of(columns):
    return columns.reshape(-1, LANES)


def on_device(
    hidden_in,
    w_query,
    query_gain,
    down_projection_matrix,
    up_projection_matrix,
    query_cotangent,
    first_moment,
    second_moment,
):
    model_width, rank = down_projection_matrix.shape
    features = up_projection_matrix.shape[1]
    chips = lax.axis_size(CHIPS)
    devices = 2 * chips
    own = (model_width + features) // devices
    height = rank * own // LANES
    packed = rank == 64 and own == LANES + 16 and model_width % LANES == 0 and chips % 4 == 0
    core = lax.axis_index("core")
    index = lax.axis_index(EVERY)
    down_t = down_projection_matrix.T
    result = backward(
        hidden_in,
        w_query,
        query_gain[None, :],
        down_t,
        up_projection_matrix,
        query_cotangent,
        first_moment.T,
        second_moment.T,
        chips,
        packed,
    )
    if packed:
        blocks, own_state = result
        params, first, second = own_state[0], own_state[1], own_state[2]
    else:
        blocks = result.reshape(rank, chips, 2, own).transpose(2, 1, 0, 3).reshape(2, chips, -1, LANES)
        combined = jnp.concatenate([down_t, up_projection_matrix], axis=1)
        params = rows_of(lax.dynamic_slice_in_dim(combined, index * own, own, 1)).astype(F32)
        first, second = rows_of(first_moment.T), rows_of(second_moment.T)

    keep = lax.dynamic_index_in_dim(blocks, core, 0, keepdims=False)
    send = lax.dynamic_index_in_dim(blocks, 1 - core, 0, keepdims=False)
    other = decoded_of(lax.ppermute(coded_of(send), "core", SWAP)) / RANGE
    coded = coded_of(keep + other)
    arrived = lax.all_to_all(coded, CHIPS, 0, 0, tiled=True)
    grads = None
    for k in range(chips):
        term = decoded_of(arrived[k])
        grads = term if grads is None else grads + term
    grads = grads / (RANGE * devices)
    first_new = beta_one * first + (1.0 - beta_one) * grads
    second_new = beta_two * second + (1.0 - beta_two) * grads * grads
    direction = first_new / first_bias / (jnp.sqrt(second_new / second_bias) + adam_eps)
    updated = (params - learn_rate * direction).astype(BF16)

    copies = jnp.broadcast_to(updated[None], (chips, height, LANES))
    copies, first_new, second_new = lax.optimization_barrier((copies, first_new, second_new))
    mine = lax.all_to_all(copies, CHIPS, 0, 0, tiled=True)
    other = lax.ppermute(mine, "core", SWAP)
    if packed:
        own_new = jnp.stack([first_new, second_new])
        down_new, up_new, first_out, second_out = finish(mine, other, own_new, model_width, features)
    else:
        pair = jnp.stack([mine, other])
        pair = jnp.where(core == 0, pair, pair[::-1])
        columns = pair.reshape(2, chips, rank, own).transpose(2, 1, 0, 3).reshape(rank, devices * own)
        down_new, up_new = columns[:, :model_width], columns[:, model_width:]
        first_out, second_out = first_new.reshape(rank, own), second_new.reshape(rank, own)
    return (down_new.T, up_new, first_out.T, second_out.T)


def solution(mesh):
    groups, replicas = mesh.shape["group"], mesh.shape["replica"]
    fine = Mesh(mesh.devices.reshape(groups, replicas // 2, 2), EVERY)
    rows = P(EVERY, None)
    return jax.shard_map(
        on_device,
        mesh=fine,
        in_specs=(rows, P(), P(), P(), P(), rows, rows, rows),
        out_specs=(P(), P(), rows, rows),
        check_vma=False,
    )
```
